32 devices in a mesh: batch: 16 (over z, y, x), rep: 2 (over core).
Axes of the slice: x: 2, y: 2, z: 4, core: 2. Of those that a mesh axis runs over, the one named last changes fastest.
Arguments:
- feats: bfloat16 [2048, 512], P('batch')
- partner: int32 [2048], P('batch'), may hold values from 0 to 2047, as said below
Outputs:
- grad: float32 [2048, 512], P('batch')
- loss: float32 [2048], P('batch')
The draws below stay inside these ranges and needn't reach their ends.
Inputs may be any that keep to these rules, and one draw needn't show every extreme that they name: partner pairs the rows: partner[partner[k]] = k and partner[k] != k.
All inputs are finite; a program needn't handle non-finite values.
Results may differ from the reference program's by a relative error of at most 0.0058.
Values may be sent and summed in bfloat16 or wider, within the bound.
No kernel may reach another device: no remote copies, remote signals or barrier semaphores. Data moves between devices by JAX's collectives and lax.ppermute only.
A program may use at most 64 MiB of HBM per device.

```python
import math
import jax
import jax.numpy as jnp
from jax import lax

D = 512
EMBS = 2048


def pairing(key):
    return jax.random.permutation(jax.random.fold_in(key, 11), EMBS).astype(jnp.int32)


def draw_partner(key, part):
    order = pairing(key)
    half = EMBS // 2
    first = order[:half]
    second = order[half:]
    result = jnp.zeros((EMBS,), jnp.int32)
    result = result.at[first].set(second)
    result = result.at[second].set(first)
    return result


def draw_feats(key, part):
    order = pairing(key)
    half = EMBS // 2
    first = order[:half]
    second = order[half:]
    classes = max(1, EMBS // 32)
    key_center = jax.random.fold_in(key, 21)
    key_class = jax.random.fold_in(key, 26)
    key_image = jax.random.fold_in(key, 27)
    key_istd = jax.random.fold_in(key, 28)
    key_vstd = jax.random.fold_in(key, 22)
    key_left = jax.random.fold_in(key, 23)
    key_right = jax.random.fold_in(key, 24)
    key_scale = jax.random.fold_in(key, 25)
    label = jax.random.randint(key_class, (half,), 0, classes)
    image_std = jnp.exp(jax.random.uniform(key_istd, (half, 1), jnp.float32, jnp.log(0.4), jnp.log(1.2)))
    view_std = jnp.exp(jax.random.uniform(key_vstd, (half, 1), jnp.float32, jnp.log(0.3), jnp.log(0.9)))
    centers = jax.random.normal(key_center, (classes, D), jnp.float32)
    image_noise = jax.random.normal(key_image, (half, D), jnp.float32)
    left = jax.random.normal(key_left, (half, D), jnp.float32)
    right = jax.random.normal(key_right, (half, D), jnp.float32)
    shared = centers[label] + image_std * image_noise
    view_one = shared + view_std * left
    view_two = shared + view_std * right
    result = jnp.zeros((EMBS, D), jnp.float32)
    result = result.at[first].set(view_one)
    result = result.at[second].set(view_two)
    row_scale = jnp.exp(jax.random.uniform(key_scale, (EMBS, 1), jnp.float32, 0.0, jnp.log(10.0)))
    return (result * row_scale).astype(jnp.bfloat16)


def setup_inputs(seed: int = 0) -> dict:
    keys = jax.random.split(jax.random.key(seed), 3)
    return {
        "feats": draw_feats(jax.random.fold_in(keys[2], 71), 0),
        "partner": draw_partner(jax.random.fold_in(keys[2], 71), 0),
    }


inv_temp = 10.0

def reference(feats, partner):
    hf = feats.astype(jnp.float32)
    scale = lax.rsqrt(lax.optimization_barrier(jnp.sum(hf * hf, axis=-1, keepdims=True)) + 1e-06)
    unit = hf * scale
    embed = unit.astype(jnp.bfloat16)
    total = embed.shape[0]
    all_ids = jnp.arange(total, dtype=jnp.int32)
    span = math.gcd(total, 512)
    starts = jnp.arange(total // span, dtype=jnp.int32) * span

    def stats(start):
        block = lax.dynamic_slice_in_dim(embed, start, span, 0)
        mates = lax.dynamic_slice_in_dim(partner, start, span, 0)
        rows = start + jnp.arange(span, dtype=jnp.int32)
        score = jnp.dot(block, embed.T, preferred_element_type=jnp.float32) * inv_temp
        weight = jnp.where(all_ids[None, :] == rows[:, None], 0.0, jnp.exp(score - inv_temp))
        pscore = lax.optimization_barrier(jnp.sum(jnp.where(all_ids[None, :] == mates[:, None], score, 0.0), axis=1))
        return (lax.optimization_barrier(jnp.sum(weight, axis=1)), pscore)
    denom, pscore = lax.map(stats, starts)
    denom = denom.reshape(total)
    pscore = pscore.reshape(total)
    lse = jnp.log(denom) + inv_temp
    loss = lse - pscore

    def grad_rows(start):
        block = lax.dynamic_slice_in_dim(embed, start, span, 0)
        mates = lax.dynamic_slice_in_dim(partner, start, span, 0)
        own_lse = lax.dynamic_slice_in_dim(lse, start, span, 0)
        rows = start + jnp.arange(span, dtype=jnp.int32)
        score = jnp.dot(block, embed.T, preferred_element_type=jnp.float32) * inv_temp
        coeff = jnp.exp(score - own_lse[:, None]) + jnp.exp(score - lse[None, :])
        coeff = coeff - 2.0 * jnp.where(all_ids[None, :] == mates[:, None], 1.0, 0.0)
        coeff = jnp.where(all_ids[None, :] == rows[:, None], 0.0, coeff).astype(jnp.bfloat16)
        return jnp.dot(coeff, embed, preferred_element_type=jnp.float32) * inv_temp
    dz = lax.map(grad_rows, starts).reshape(total, embed.shape[1])
    grad = scale * (dz - unit * lax.optimization_barrier(jnp.sum(unit * dz, axis=-1, keepdims=True)))
    return (grad, loss)
```

```python
import functools
import math

import jax
import jax.numpy as jnp
from jax import lax
from jax.experimental import pallas as pl
from jax.experimental.pallas import tpu as pltpu
from jax.sharding import PartitionSpec as P

inv_temp = 10.0
log2e = 1.4426950408889634


def split_plan(feats, partner):
    rows, width = feats.shape
    layers = lax.axis_size("rep")
    share = rows // layers
    layer = lax.axis_index("rep")
    block_index = lax.axis_index("batch")
    hf = feats.astype(jnp.float32)
    scale = lax.rsqrt(jnp.sum(hf * hf, axis=-1, keepdims=True) + 1e-06)
    unit = hf * scale
    embed = unit.astype(jnp.bfloat16)
    own_ids = block_index * rows + jnp.arange(rows, dtype=jnp.int32)
    mine = lax.dynamic_slice_in_dim(embed, layer * share, share, 0)

    def key_ids(start, count):
        gathered = start + jnp.arange(count, dtype=jnp.int32)
        return gathered // share * rows + layer * share + gathered % share

    def first_fold(carry, piece, start):
        denom, pscore = carry
        score = jnp.dot(embed, piece.T, preferred_element_type=jnp.float32) * inv_temp
        ids = key_ids(start, piece.shape[0])
        weight = jnp.where(ids[None, :] == own_ids[:, None], 0.0, jnp.exp(score - inv_temp))
        hits = jnp.where(ids[None, :] == partner[:, None], score, 0.0)
        return (denom + jnp.sum(weight, axis=1), pscore + jnp.sum(hits, axis=1))

    empty_rows = jnp.zeros((rows,), jnp.float32)
    keys = lax.all_gather(mine, "batch", axis=0, tiled=True)
    group = math.gcd(lax.axis_size("batch"), max(1, 512 // share))
    span = group * share
    turns = keys.shape[0] // span
    stacked = keys.reshape(turns, span, width)
    starts = jnp.arange(turns, dtype=jnp.int32) * span

    def first_step(carry, item):
        return (first_fold(carry, item[0], item[1]), None)

    (denom, pscore), unused = lax.scan(first_step, (empty_rows, empty_rows), (stacked, starts))
    denom, pscore = lax.psum((denom, pscore), "rep")
    lse = jnp.log(denom) + inv_temp
    loss = lse - pscore
    lse_share = lax.dynamic_slice_in_dim(lse, layer * share, share, 0)

    def second_fold(acc, pieces, start):
        piece, piece_lse = pieces
        score = jnp.dot(embed, piece.T, preferred_element_type=jnp.float32) * inv_temp
        ids = key_ids(start, piece.shape[0])
        coeff = jnp.exp(score - lse[:, None]) + jnp.exp(score - piece_lse[None, :])
        coeff = coeff - 2.0 * jnp.where(ids[None, :] == partner[:, None], 1.0, 0.0)
        coeff = jnp.where(ids[None, :] == own_ids[:, None], 0.0, coeff).astype(jnp.bfloat16)
        return acc + jnp.dot(coeff, piece, preferred_element_type=jnp.float32)

    empty_acc = jnp.zeros((rows, width), jnp.float32)
    key_lse = lax.all_gather(lse_share, "batch", axis=0, tiled=True)
    stacked_lse = key_lse.reshape(turns, span)

    def second_step(acc, item):
        return (second_fold(acc, (item[0], item[1]), item[2]), None)

    acc, unused = lax.scan(second_step, empty_acc, (stacked, stacked_lse, starts))
    part_sum = lax.psum_scatter(acc, "rep", scatter_dimension=0, tiled=True)
    dz_share = part_sum * inv_temp
    unit_share = lax.dynamic_slice_in_dim(unit, layer * share, share, 0)
    scale_share = lax.dynamic_slice_in_dim(scale, layer * share, share, 0)
    grad_share = scale_share * (
        dz_share - unit_share * jnp.sum(unit_share * dz_share, axis=-1, keepdims=True)
    )
    grad = lax.all_gather(grad_share, "rep", axis=0, tiled=True)
    return (grad, loss)


X, Y, XY, Z1, Z2, Z3 = 1, 2, 3, 4, 8, 12


def send(piece, first, second=None):
    offsets = (first, first if second is None else second)
    pairs = [
        (2 * b + c, 2 * (b ^ offsets[c]) + c) for b in range(lax.axis_size("batch")) for c in range(2)
    ]
    return lax.ppermute(piece, ("batch", "rep"), pairs)


def swap(piece):
    return lax.ppermute(piece, "rep", [(0, 1), (1, 0)])


def join(*pieces):
    return jnp.concatenate(pieces, axis=0)


def gather_halves(half):
    z1, z2, z3 = send(half, Z1), send(half, Z2), send(half, Z3)
    near = join(half, z1)
    near_x, near_y, near_xy = send(near, X, Y), send(near, Y, X), send(near, XY)
    far = join(z2, z3)
    far_x, far_y, far_xy = send(far, X, Y), send(far, Y, X), send(far, XY)
    n, f = (0, Z1), (Z2, Z3)
    mine = [
        (join(z1, near_x, near_y, near_xy), (Z1, *(X ^ o for o in n), *(Y ^ o for o in n), *(XY ^ o for o in n))),
        (join(far, far_x, far_y), (*f, *(X ^ o for o in f), *(Y ^ o for o in f))),
        (far_xy, tuple(XY ^ o for o in f)),
    ]
    return mine, [(swap(piece), offsets) for piece, offsets in mine]


def score_kernel(n_pieces, own_ref, mate_ref, *refs):
    pieces = refs[:n_pieces]
    grad_ref, loss_ref, embed, weights, col_denom = refs[n_pieces:]
    rows, width = own_ref.shape
    total = embed.shape[0]
    block = 2 * rows
    blocks = total // block

    def normalized(raw):
        hf = raw.astype(jnp.float32)
        scale = lax.rsqrt(jnp.sum(hf * hf, axis=-1, keepdims=True) + 1e-06)
        return hf * scale, scale

    start = 0
    for ref in (own_ref, *pieces):
        count = ref.shape[0]
        for at in range(0, count, 64):
            embed[start + at : start + at + 64, :] = normalized(ref[at : at + 64, :])[0].astype(jnp.bfloat16)
        start += count

    col_denom[...] = jnp.zeros_like(col_denom)
    mates = mate_ref[...]
    own_denom = jnp.zeros((rows, 128), jnp.float32)
    own_hits = jnp.zeros((rows, 128), jnp.float32)
    for i in range(blocks):
        left = embed[i * block : (i + 1) * block, :]
        row_sum = jnp.zeros((block, 128), jnp.float32)
        for j in range(i, blocks):
            right = embed[j * block : (j + 1) * block, :]
            score = lax.dot_general(left, right, (((1,), (1,)), ((), ())), preferred_element_type=jnp.float32)
            weight = jnp.exp2(score * (inv_temp * log2e))
            if i == j:
                r = lax.broadcasted_iota(jnp.int32, (block, block), 0)
                c = lax.broadcasted_iota(jnp.int32, (block, block), 1)
                weight = jnp.where(r == c, 0.0, weight)
            if i == 0:
                top = weight[:rows]
                weights[:, j * block : (j + 1) * block] = top
                ids = j * block + lax.broadcasted_iota(jnp.int32, (rows, block), 1)
                hits = jnp.where(ids == mates, score[:rows], 0.0)
                for k in range(0, block, 128):
                    own_denom += top[:, k : k + 128]
                    own_hits += hits[:, k : k + 128]
            cols = jnp.sum(weight.reshape(block // 8, 8, block), axis=0)
            col_denom[:, j * block : (j + 1) * block] += cols
            if i != j:
                for k in range(0, block, 128):
                    row_sum += weight[:, k : k + 128]
        if i != blocks - 1:
            cols = jnp.sum(row_sum.T.reshape(16, 8, block), axis=0)
            col_denom[:, i * block : (i + 1) * block] += cols

    own = jnp.sum(own_denom, axis=1, keepdims=True)
    loss_ref[...] = jnp.log(own) - inv_temp * jnp.sum(own_hits, axis=1, keepdims=True)
    own_inverse = 1.0 / own
    dz = jnp.zeros((rows, width), jnp.float32)
    for j in range(blocks):
        cols = slice(j * block, (j + 1) * block)
        inverse = 1.0 / jnp.sum(col_denom[:, cols], axis=0, keepdims=True)
        ids = j * block + lax.broadcasted_iota(jnp.int32, (rows, block), 1)
        coeff = weights[:, cols] * (own_inverse + inverse) - jnp.where(ids == mates, 2.0, 0.0)
        dz += jnp.dot(coeff.astype(jnp.bfloat16), embed[cols, :], preferred_element_type=jnp.float32)
    dz = dz * inv_temp
    unit, scale = normalized(own_ref[...])
    grad_ref[...] = scale * (dz - unit * jnp.sum(unit * dz, axis=-1, keepdims=True))


def whole_plan(feats, partner):
    rows, width = feats.shape
    share = rows // 2
    layer = lax.axis_index("rep")
    half = lax.dynamic_slice_in_dim(feats, layer * share, share, 0)
    mine, other = gather_halves(half)
    slots = [o for _, offsets in mine for o in offsets]
    total = rows * lax.axis_size("batch")

    offset = partner // rows ^ lax.axis_index("batch")
    within = partner % rows
    part = within // share
    turned = jnp.where(part == 0, offset, offset & ~3 | (offset & 1) << 1 | (offset & 2) >> 1)
    slot = jnp.sum(
        jnp.where(turned[:, None] == jnp.array(slots, jnp.int32)[None, :], jnp.arange(len(slots), dtype=jnp.int32)[None, :], 0), axis=1
    )
    first = rows + jnp.where(part == layer, 0, len(slots) * share)
    mate = jnp.where(offset == 0, within, first + slot * share + within % share)

    pieces = [piece for piece, _ in mine + other]
    vmem = pl.BlockSpec(memory_space=pltpu.VMEM)
    grad, loss = pl.pallas_call(
        functools.partial(score_kernel, len(pieces)),
        out_shape=(
            jax.ShapeDtypeStruct((rows, width), jnp.float32),
            jax.ShapeDtypeStruct((rows, 1), jnp.float32),
        ),
        in_specs=[vmem] * (2 + len(pieces)),
        out_specs=(vmem, vmem),
        scratch_shapes=[
            pltpu.VMEM((total, width), jnp.bfloat16),
            pltpu.VMEM((rows, total), jnp.float32),
            pltpu.VMEM((8, total), jnp.float32),
        ],
        compiler_params=pltpu.CompilerParams(vmem_limit_bytes=32 * 1024 * 1024),
    )(feats, mate[:, None], *pieces)
    return grad, loss[:, 0]


def solution(mesh):
    whole = mesh.shape["batch"] == 16 and mesh.shape["rep"] == 2
    in_specs = (P("batch", None), P("batch"))
    out_specs = (P("batch", None), P("batch"))
    return jax.shard_map(
        whole_plan if whole else split_plan, mesh=mesh, in_specs=in_specs, out_specs=out_specs, check_vma=False
    )
```

```python
import functools
import math

import jax
import jax.numpy as jnp
from jax import lax
from jax.experimental import pallas as pl
from jax.experimental.pallas import tpu as pltpu
from jax.sharding import PartitionSpec as P

inv_temp = 10.0
log2e = 1.4426950408889634


def split_plan(feats, partner):
    rows, width = feats.shape
    layers = lax.axis_size("rep")
    share = rows // layers
    layer = lax.axis_index("rep")
    block_index = lax.axis_index("batch")
    hf = feats.astype(jnp.float32)
    scale = lax.rsqrt(jnp.sum(hf * hf, axis=-1, keepdims=True) + 1e-06)
    unit = hf * scale
    embed = unit.astype(jnp.bfloat16)
    own_ids = block_index * rows + jnp.arange(rows, dtype=jnp.int32)
    mine = lax.dynamic_slice_in_dim(embed, layer * share, share, 0)

    def key_ids(start, count):
        gathered = start + jnp.arange(count, dtype=jnp.int32)
        return gathered // share * rows + layer * share + gathered % share

    def first_fold(carry, piece, start):
        denom, pscore = carry
        score = jnp.dot(embed, piece.T, preferred_element_type=jnp.float32) * inv_temp
        ids = key_ids(start, piece.shape[0])
        weight = jnp.where(ids[None, :] == own_ids[:, None], 0.0, jnp.exp(score - inv_temp))
        hits = jnp.where(ids[None, :] == partner[:, None], score, 0.0)
        return (denom + jnp.sum(weight, axis=1), pscore + jnp.sum(hits, axis=1))

    empty_rows = jnp.zeros((rows,), jnp.float32)
    keys = lax.all_gather(mine, "batch", axis=0, tiled=True)
    group = math.gcd(lax.axis_size("batch"), max(1, 512 // share))
    span = group * share
    turns = keys.shape[0] // span
    stacked = keys.reshape(turns, span, width)
    starts = jnp.arange(turns, dtype=jnp.int32) * span

    def first_step(carry, item):
        return (first_fold(carry, item[0], item[1]), None)

    (denom, pscore), unused = lax.scan(first_step, (empty_rows, empty_rows), (stacked, starts))
    denom, pscore = lax.psum((denom, pscore), "rep")
    lse = jnp.log(denom) + inv_temp
    loss = lse - pscore
    lse_share = lax.dynamic_slice_in_dim(lse, layer * share, share, 0)

    def second_fold(acc, pieces, start):
        piece, piece_lse = pieces
        score = jnp.dot(embed, piece.T, preferred_element_type=jnp.float32) * inv_temp
        ids = key_ids(start, piece.shape[0])
        coeff = jnp.exp(score - lse[:, None]) + jnp.exp(score - piece_lse[None, :])
        coeff = coeff - 2.0 * jnp.where(ids[None, :] == partner[:, None], 1.0, 0.0)
        coeff = jnp.where(ids[None, :] == own_ids[:, None], 0.0, coeff).astype(jnp.bfloat16)
        return acc + jnp.dot(coeff, piece, preferred_element_type=jnp.float32)

    empty_acc = jnp.zeros((rows, width), jnp.float32)
    key_lse = lax.all_gather(lse_share, "batch", axis=0, tiled=True)
    stacked_lse = key_lse.reshape(turns, span)

    def second_step(acc, item):
        return (second_fold(acc, (item[0], item[1]), item[2]), None)

    acc, unused = lax.scan(second_step, empty_acc, (stacked, stacked_lse, starts))
    part_sum = lax.psum_scatter(acc, "rep", scatter_dimension=0, tiled=True)
    dz_share = part_sum * inv_temp
    unit_share = lax.dynamic_slice_in_dim(unit, layer * share, share, 0)
    scale_share = lax.dynamic_slice_in_dim(scale, layer * share, share, 0)
    grad_share = scale_share * (
        dz_share - unit_share * jnp.sum(unit_share * dz_share, axis=-1, keepdims=True)
    )
    grad = lax.all_gather(grad_share, "rep", axis=0, tiled=True)
    return (grad, loss)


X, Y, XY, Z1, Z2, Z3 = 1, 2, 3, 4, 8, 12


def send(piece, first, second=None):
    offsets = (first, first if second is None else second)
    pairs = [
        (2 * b + c, 2 * (b ^ offsets[c]) + c) for b in range(lax.axis_size("batch")) for c in range(2)
    ]
    return lax.ppermute(piece, ("batch", "rep"), pairs)


def swap(piece):
    return lax.ppermute(piece, "rep", [(0, 1), (1, 0)])


def join(*pieces):
    return jnp.concatenate(pieces, axis=0)


class Chunk:
    def __init__(self, offsets, parts=None):
        self.offsets = offsets
        self.parts = parts

    def swapped(self):
        return Chunk(self.offsets[::-1], self.parts and self.parts[::-1])


def halves(first, second, *within):
    return [Chunk((first ^ w, second ^ w), (0, 1)) for w in within]


def whole(first, second):
    return [Chunk((first, second))]


def gather_rows(feats):
    far = send(feats, Z2, Z3)
    near = send(feats, X, Y)
    cross = send(feats, XY, Z1)
    side = send(near, Z1)
    side_xy = send(cross, Z1, XY)
    far_x, far_y = send(far, X, Y), send(far, Y, X)
    far_xy = send(far, XY)

    def both(piece, chunks):
        return [(piece, chunks), (swap(piece), [chunk.swapped() for chunk in chunks])]

    early = both(join(near, cross, far), whole(X, Y) + whole(XY, Z1) + whole(Z2, Z3))
    middle = both(side, whole(X ^ Z1, Y ^ Z1))
    late = both(join(far_x, far_y), whole(X ^ Z2, Y ^ Z3) + whole(Y ^ Z2, X ^ Z3))
    last = both(far_xy, whole(XY ^ Z2, XY ^ Z3))
    return [[(feats, whole(0, 0))] + early, middle + late + last + [(side_xy, whole(XY ^ Z1, XY ^ Z1))]]


def normalized(raw):
    hf = raw.astype(jnp.float32)
    scale = lax.rsqrt(jnp.sum(hf * hf, axis=-1, keepdims=True) + 1e-06)
    return hf * scale, scale


def normalize_into(embed, refs):
    start = 0
    for ref in refs:
        count = ref.shape[0]
        for at in range(0, count, 64):
            embed[start + at : start + at + 64, :] = normalized(ref[at : at + 64, :])[0].astype(jnp.bfloat16)
        start += count


def partner_column(partner_ref):
    rows = partner_ref.shape[1]
    spread = jnp.broadcast_to(partner_ref[...], (rows, rows)).astype(jnp.float32)
    return jnp.sum(jnp.where(diagonal(rows), spread, 0.0), axis=1, keepdims=True).astype(jnp.int32)


def diagonal(size):
    r = lax.broadcasted_iota(jnp.int32, (size, size), 0)
    c = lax.broadcasted_iota(jnp.int32, (size, size), 1)
    return r == c


def column_ids(chunks, rows):
    layer = lax.axis_index("rep")
    block = lax.axis_index("batch")
    lane = lax.broadcasted_iota(jnp.int32, (1, rows), 1)
    share = rows // 2

    def base(chunk):
        first = (block ^ jnp.where(layer == 0, *chunk.offsets)) * rows
        return first if chunk.parts is None else first + jnp.where(layer == 0, *chunk.parts) * share

    ids = []
    waiting = []
    for chunk in chunks:
        if chunk.parts is None:
            ids.append(lane + base(chunk))
        else:
            waiting.append(base(chunk))
        if len(waiting) == 2:
            ids.append(lane + jnp.where(lane < share, waiting[0], waiting[1] - share))
            waiting = []
    return ids


def spans(total, block):
    return [slice(start, min(start + block, total)) for start in range(0, total, block)]


def shift(span, by):
    return slice(span.start + by, span.stop + by)


def weigh(left, right):
    score = lax.dot_general(left, right, (((1,), (1,)), ((), ())), preferred_element_type=jnp.float32)
    return score, jnp.exp2(score * (inv_temp * log2e))


def fold_rows(weight):
    return jnp.sum(weight.reshape(weight.shape[0] // 8, 8, weight.shape[1]), axis=0)


def fold_columns(weight):
    return sum(weight[:, k : k + 128] for k in range(0, weight.shape[1], 128))


def triangle(embed, total, block, denom, top):
    blocks = total // block
    for i in range(blocks):
        left = embed[i * block : (i + 1) * block, :]
        row_sum = jnp.zeros((block, 128), jnp.float32)
        for j in range(i, blocks):
            score, weight = weigh(left, embed[j * block : (j + 1) * block, :])
            if i == j:
                weight = jnp.where(diagonal(block), 0.0, weight)
            else:
                row_sum += fold_columns(weight)
            if i == 0:
                top(j, score, weight)
            denom[:, j * block : (j + 1) * block] += fold_rows(weight)
        if i != blocks - 1:
            denom[:, i * block : (i + 1) * block] += fold_rows(row_sum.T)


def stage_kernel(chunks, final, partner_ref, own_ref, *refs):
    before = chunks[:-1]
    refs = list(refs)

    def take(count):
        taken = refs[:count]
        del refs[:count]
        return taken

    old_embeds = take(len(before))
    old_weights = take(len(before)) if final else []
    old_denom, old_hits = take(2) if before else (None, None)
    if final:
        grad_ref, loss_ref, embed, weights, denom = refs[-5:]
        pieces = refs[:-5]
    else:
        embed, weights, denom, hits_ref = refs[-4:]
        pieces = refs[:-4]
    rows, width = own_ref.shape
    block = 2 * rows
    new = embed.shape[0]
    old = denom.shape[1] - new

    normalize_into(embed, pieces)
    mates = partner_column(partner_ref)
    ids = [column_ids(part, rows) for part in chunks]
    hits = old_hits[...] if before else jnp.zeros((rows, rows), jnp.float32)
    if before:
        denom[:, :old] = old_denom[...]
    denom[:, old:] = jnp.zeros((8, new), jnp.float32)

    def is_mate(names, span):
        return [name == mates for name in names[span.start // rows : span.stop // rows]]

    def found(span, score):
        return sum(
            jnp.where(mate, score[:rows, k * rows : (k + 1) * rows], 0.0)
            for k, mate in enumerate(is_mate(ids[-1], span))
        )

    start = 0
    for old_embed in old_embeds:
        for i in spans(old_embed.shape[0], block):
            left = old_embed[i, :]
            row_sum = jnp.zeros((left.shape[0], 128), jnp.float32)
            for j in spans(new, block):
                score, weight = weigh(left, embed[j, :])
                if start + i.start == 0:
                    weights[:, j] = weight[:rows]
                    hits += found(j, score)
                row_sum += fold_columns(weight)
                denom[:, shift(j, old)] += fold_rows(weight)
            denom[:, shift(i, start)] += fold_rows(row_sum.T)
        start += old_embed.shape[0]
    for i in spans(new, block):
        left = embed[i, :]
        row_sum = jnp.zeros((left.shape[0], 128), jnp.float32)
        for j in spans(new, block):
            if j.start < i.start:
                continue
            score, weight = weigh(left, embed[j, :])
            if i == j:
                weight = jnp.where(diagonal(weight.shape[0]), 0.0, weight)
            else:
                row_sum += fold_columns(weight)
            if not before and i.start == 0:
                weights[:, j] = weight[:rows]
                hits += found(j, score)
            denom[:, shift(j, old)] += fold_rows(weight)
        if i.stop != new:
            denom[:, shift(i, old)] += fold_rows(row_sum.T)
    if not final:
        hits_ref[...] = hits
        return

    all_weights = [*old_weights, weights]
    own = jnp.sum(sum(fold_columns(w[...]) for w in all_weights), axis=1, keepdims=True)
    loss = jnp.log(own) - inv_temp * jnp.sum(hits, axis=1, keepdims=True)
    loss_ref[...] = jnp.sum(jnp.where(diagonal(rows), loss, 0.0), axis=0, keepdims=True)
    own_inverse = 1.0 / own
    dz = jnp.zeros((rows, width), jnp.float32)
    start = 0
    for e, w, names in zip([*old_embeds, embed], all_weights, ids):
        for j in spans(e.shape[0], block):
            inverse = 1.0 / jnp.sum(denom[:, shift(j, start)], axis=0, keepdims=True)
            mate = jnp.concatenate(is_mate(names, j), axis=1)
            coeff = w[:, j] * (own_inverse + inverse) - jnp.where(mate, 2.0, 0.0)
            dz += jnp.dot(coeff.astype(jnp.bfloat16), e[j, :], preferred_element_type=jnp.float32)
        start += e.shape[0]
    dz = dz * inv_temp
    unit, scale = normalized(own_ref[...])
    grad_ref[...] = scale * (dz - unit * jnp.sum(unit * dz, axis=-1, keepdims=True))


def whole_plan(feats, partner):
    rows, width = feats.shape
    stages = gather_rows(feats)
    mates = partner[None, :]
    f32, bf16 = jnp.float32, jnp.bfloat16
    vmem = pl.BlockSpec(memory_space=pltpu.VMEM)
    chunks, embeds, weights, sums = [], [], [], []
    done = 0
    for s, stage in enumerate(stages):
        if callable(stage):
            stage = stage(sums)
        pieces = [piece for piece, _ in stage]
        chunks.append([chunk for _, part in stage for chunk in part])
        new = sum(piece.shape[0] for piece in pieces)
        state = [((new, width), bf16), ((rows, new), f32), ((8, done + new), f32)]
        final = s == len(stages) - 1
        outs = [((rows, width), f32), ((1, rows), f32)] if final else state + [((rows, rows), f32)]
        operands = [mates, feats, *embeds, *(weights if final else []), *sums, *pieces]
        results = pl.pallas_call(
            functools.partial(stage_kernel, list(chunks), final),
            out_shape=tuple(jax.ShapeDtypeStruct(shape, dtype) for shape, dtype in outs),
            in_specs=[vmem] * len(operands),
            out_specs=(vmem,) * len(outs),
            scratch_shapes=[pltpu.VMEM(shape, dtype) for shape, dtype in (state if final else [])],
            cost_estimate=pl.CostEstimate(flops=new * (2 * done + new) * width, bytes_accessed=0, transcendentals=0),
            compiler_params=pltpu.CompilerParams(vmem_limit_bytes=32 * 1024 * 1024),
        )(*operands)
        if not final:
            embeds.append(results[0])
            weights.append(results[1])
            sums = list(results[2:])
        done += new
    grad, loss = results
    return grad, loss.reshape(rows)


def solution(mesh):
    every = mesh.shape["batch"] == 16 and mesh.shape["rep"] == 2
    in_specs = (P("batch", None), P("batch"))
    out_specs = (P("batch", None), P("batch"))
    return jax.shard_map(
        whole_plan if every else split_plan, mesh=mesh, in_specs=in_specs, out_specs=out_specs, check_vma=False
    )
```

```python
import functools
import math

import jax
import jax.numpy as jnp
from jax import lax
from jax.experimental import pallas as pl
from jax.experimental.pallas import tpu as pltpu
from jax.sharding import PartitionSpec as P

inv_temp = 10.0
log2e = 1.4426950408889634


def split_plan(feats, partner):
    rows, width = feats.shape
    layers = lax.axis_size("rep")
    share = rows // layers
    layer = lax.axis_index("rep")
    block_index = lax.axis_index("batch")
    hf = feats.astype(jnp.float32)
    scale = lax.rsqrt(jnp.sum(hf * hf, axis=-1, keepdims=True) + 1e-06)
    unit = hf * scale
    embed = unit.astype(jnp.bfloat16)
    own_ids = block_index * rows + jnp.arange(rows, dtype=jnp.int32)
    mine = lax.dynamic_slice_in_dim(embed, layer * share, share, 0)

    def key_ids(start, count):
        gathered = start + jnp.arange(count, dtype=jnp.int32)
        return gathered // share * rows + layer * share + gathered % share

    def first_fold(carry, piece, start):
        denom, pscore = carry
        score = jnp.dot(embed, piece.T, preferred_element_type=jnp.float32) * inv_temp
        ids = key_ids(start, piece.shape[0])
        weight = jnp.where(ids[None, :] == own_ids[:, None], 0.0, jnp.exp(score - inv_temp))
        hits = jnp.where(ids[None, :] == partner[:, None], score, 0.0)
        return (denom + jnp.sum(weight, axis=1), pscore + jnp.sum(hits, axis=1))

    empty_rows = jnp.zeros((rows,), jnp.float32)
    keys = lax.all_gather(mine, "batch", axis=0, tiled=True)
    group = math.gcd(lax.axis_size("batch"), max(1, 512 // share))
    span = group * share
    turns = keys.shape[0] // span
    stacked = keys.reshape(turns, span, width)
    starts = jnp.arange(turns, dtype=jnp.int32) * span

    def first_step(carry, item):
        return (first_fold(carry, item[0], item[1]), None)

    (denom, pscore), unused = lax.scan(first_step, (empty_rows, empty_rows), (stacked, starts))
    denom, pscore = lax.psum((denom, pscore), "rep")
    lse = jnp.log(denom) + inv_temp
    loss = lse - pscore
    lse_share = lax.dynamic_slice_in_dim(lse, layer * share, share, 0)

    def second_fold(acc, pieces, start):
        piece, piece_lse = pieces
        score = jnp.dot(embed, piece.T, preferred_element_type=jnp.float32) * inv_temp
        ids = key_ids(start, piece.shape[0])
        coeff = jnp.exp(score - lse[:, None]) + jnp.exp(score - piece_lse[None, :])
        coeff = coeff - 2.0 * jnp.where(ids[None, :] == partner[:, None], 1.0, 0.0)
        coeff = jnp.where(ids[None, :] == own_ids[:, None], 0.0, coeff).astype(jnp.bfloat16)
        return acc + jnp.dot(coeff, piece, preferred_element_type=jnp.float32)

    empty_acc = jnp.zeros((rows, width), jnp.float32)
    key_lse = lax.all_gather(lse_share, "batch", axis=0, tiled=True)
    stacked_lse = key_lse.reshape(turns, span)

    def second_step(acc, item):
        return (second_fold(acc, (item[0], item[1]), item[2]), None)

    acc, unused = lax.scan(second_step, empty_acc, (stacked, stacked_lse, starts))
    part_sum = lax.psum_scatter(acc, "rep", scatter_dimension=0, tiled=True)
    dz_share = part_sum * inv_temp
    unit_share = lax.dynamic_slice_in_dim(unit, layer * share, share, 0)
    scale_share = lax.dynamic_slice_in_dim(scale, layer * share, share, 0)
    grad_share = scale_share * (
        dz_share - unit_share * jnp.sum(unit_share * dz_share, axis=-1, keepdims=True)
    )
    grad = lax.all_gather(grad_share, "rep", axis=0, tiled=True)
    return (grad, loss)


X, Y, XY, Z1, Z2, Z3 = 1, 2, 3, 4, 8, 12


def send(piece, first, second=None):
    offsets = (first, first if second is None else second)
    pairs = [
        (2 * b + c, 2 * (b ^ offsets[c]) + c) for b in range(lax.axis_size("batch")) for c in range(2)
    ]
    return lax.ppermute(piece, ("batch", "rep"), pairs)


def swap(piece):
    return lax.ppermute(piece, "rep", [(0, 1), (1, 0)])


def join(*pieces):
    return jnp.concatenate(pieces, axis=0)


class Chunk:
    def __init__(self, offsets, parts=None):
        self.offsets = offsets
        self.parts = parts

    def swapped(self):
        return Chunk(self.offsets[::-1], self.parts and self.parts[::-1])


def halves(first, second, *within):
    return [Chunk((first ^ w, second ^ w), (0, 1)) for w in within]


def whole(first, second):
    return [Chunk((first, second))]


def gather_rows(feats):
    far = send(feats, Z2, Z3)
    near = send(feats, X, Y)
    cross = send(feats, XY, Z1)
    side = send(near, Z1)
    side_xy = send(cross, Z1, XY)
    far_x, far_y = send(far, X, Y), send(far, Y, X)
    far_xy = send(far_x, Y, X)

    def both(piece, chunks):
        return [(piece, chunks), (swap(piece), [chunk.swapped() for chunk in chunks])]

    def split(piece, first, second):
        share = piece.shape[0] // 2
        halves = [(swap(piece[k * share : (k + 1) * share]), [Chunk((second, first), (k, k))]) for k in range(2)]
        return [(piece, whole(first, second))] + halves

    early = both(join(near, cross, far), whole(X, Y) + whole(XY, Z1) + whole(Z2, Z3))

    def late():
        return both(join(far_x, far_y), whole(X ^ Z2, Y ^ Z3) + whole(Y ^ Z2, X ^ Z3))

    def last(sums):
        g, s, sx, hits = lax.optimization_barrier((far_xy, side, side_xy, sums[1]))
        sums = [sums[0], hits]
        return late() + both(s, whole(X ^ Z1, Y ^ Z1)) + both(g, whole(XY ^ Z2, XY ^ Z3)) + [(sx, whole(XY ^ Z1, XY ^ Z1))], sums

    return [[(feats, whole(0, 0))] + early, last]


def normalized(raw):
    hf = raw.astype(jnp.float32)
    scale = lax.rsqrt(jnp.sum(hf * hf, axis=-1, keepdims=True) + 1e-06)
    return hf * scale, scale


def normalize_into(embed, refs):
    start = 0
    for ref in refs:
        count = ref.shape[0]
        for at in range(0, count, 64):
            embed[start + at : start + at + 64, :] = normalized(ref[at : at + 64, :])[0].astype(jnp.bfloat16)
        start += count


def partner_column(partner_ref):
    rows = partner_ref.shape[1]
    spread = jnp.broadcast_to(partner_ref[...], (rows, rows)).astype(jnp.float32)
    return jnp.sum(jnp.where(diagonal(rows), spread, 0.0), axis=1, keepdims=True).astype(jnp.int32)


def diagonal(size):
    r = lax.broadcasted_iota(jnp.int32, (size, size), 0)
    c = lax.broadcasted_iota(jnp.int32, (size, size), 1)
    return r == c


def column_ids(chunks, rows):
    layer = lax.axis_index("rep")
    block = lax.axis_index("batch")
    lane = lax.broadcasted_iota(jnp.int32, (1, rows), 1)
    share = rows // 2

    def base(chunk):
        first = (block ^ jnp.where(layer == 0, *chunk.offsets)) * rows
        return first if chunk.parts is None else first + jnp.where(layer == 0, *chunk.parts) * share

    groups = {}
    start = 0
    for chunk in chunks:
        stop = start + (rows if chunk.parts is None else share)
        for group in range(start // rows, (stop - 1) // rows + 1):
            value = lane + (base(chunk) + group * rows - start)
            before = groups.get(group)
            groups[group] = value if before is None else jnp.where(lane < start - group * rows, before, value)
        start = stop
    return [groups[group] for group in range(start // rows)]


def spans(total, block):
    return [slice(start, min(start + block, total)) for start in range(0, total, block)]


def shift(span, by):
    return slice(span.start + by, span.stop + by)


def weigh(left, right):
    score = lax.dot_general(left, right, (((1,), (1,)), ((), ())), preferred_element_type=jnp.float32)
    return score, jnp.exp2(score * (inv_temp * log2e))


def fold_rows(weight):
    return jnp.sum(weight.reshape(weight.shape[0] // 8, 8, weight.shape[1]), axis=0)


def fold_columns(weight):
    return sum(weight[:, k : k + 128] for k in range(0, weight.shape[1], 128))


def triangle(embed, total, block, denom, top):
    blocks = total // block
    for i in range(blocks):
        left = embed[i * block : (i + 1) * block, :]
        row_sum = jnp.zeros((block, 128), jnp.float32)
        for j in range(i, blocks):
            score, weight = weigh(left, embed[j * block : (j + 1) * block, :])
            if i == j:
                weight = jnp.where(diagonal(block), 0.0, weight)
            else:
                row_sum += fold_columns(weight)
            if i == 0:
                top(j, score, weight)
            denom[:, j * block : (j + 1) * block] += fold_rows(weight)
        if i != blocks - 1:
            denom[:, i * block : (i + 1) * block] += fold_rows(row_sum.T)


def stage_kernel(chunks, final, partner_ref, own_ref, *refs):
    before = chunks[:-1]
    refs = list(refs)

    def take(count):
        taken = refs[:count]
        del refs[:count]
        return taken

    old_embeds = take(len(before))
    old_weights = take(len(before)) if final else []
    old_denom, old_hits = take(2) if before else (None, None)
    if final:
        grad_ref, loss_ref, embed, weights, denom = refs[-5:]
        pieces = refs[:-5]
    else:
        embed, weights, denom, hits_ref = refs[-4:]
        pieces = refs[:-4]
    rows, width = own_ref.shape
    block = 2 * rows
    new = embed.shape[0]
    old = denom.shape[1] - new

    normalize_into(embed, pieces)
    mates = partner_column(partner_ref)
    ids = [column_ids(part, rows) for part in chunks]
    hits = old_hits[...] if before else jnp.zeros((rows, rows), jnp.float32)
    if before:
        denom[:, :old] = old_denom[...]
    denom[:, old:] = jnp.zeros((8, new), jnp.float32)

    def is_mate(names, span):
        return [name == mates for name in names[span.start // rows : span.stop // rows]]

    def found(span, score):
        return sum(
            jnp.where(mate, score[:rows, k * rows : (k + 1) * rows], 0.0)
            for k, mate in enumerate(is_mate(ids[-1], span))
        )

    start = 0
    for old_embed in old_embeds:
        for i in spans(old_embed.shape[0], 2 * block):
            left = old_embed[i, :]
            row_sum = jnp.zeros((left.shape[0], 128), jnp.float32)
            for j in spans(new, block):
                score, weight = weigh(left, embed[j, :])
                if start + i.start == 0:
                    weights[:, j] = weight[:rows]
                    hits += found(j, score)
                row_sum += fold_columns(weight)
                denom[:, shift(j, old)] += fold_rows(weight)
            denom[:, shift(i, start)] += fold_rows(row_sum.T)
        start += old_embed.shape[0]
    for i in spans(new, block):
        left = embed[i, :]
        row_sum = jnp.zeros((left.shape[0], 128), jnp.float32)
        for j in spans(new, block):
            if j.start < i.start:
                continue
            score, weight = weigh(left, embed[j, :])
            if i == j:
                weight = jnp.where(diagonal(weight.shape[0]), 0.0, weight)
            else:
                row_sum += fold_columns(weight)
            if not before and i.start == 0:
                weights[:, j] = weight[:rows]
                hits += found(j, score)
            denom[:, shift(j, old)] += fold_rows(weight)
        if i.stop != new:
            denom[:, shift(i, old)] += fold_rows(row_sum.T)
    if not final:
        hits_ref[...] = hits
        return

    all_weights = [*old_weights, weights]
    own = jnp.sum(sum(fold_columns(w[...]) for w in all_weights), axis=1, keepdims=True)
    loss = jnp.log(own) - inv_temp * jnp.sum(hits, axis=1, keepdims=True)
    loss_ref[...] = jnp.sum(jnp.where(diagonal(rows), loss, 0.0), axis=0, keepdims=True)
    own_inverse = 1.0 / own
    dz = jnp.zeros((rows, width), jnp.float32)
    start = 0
    for e, w, names in zip([*old_embeds, embed], all_weights, ids):
        for j in spans(e.shape[0], block):
            inverse = 1.0 / jnp.sum(denom[:, shift(j, start)], axis=0, keepdims=True)
            mate = jnp.concatenate(is_mate(names, j), axis=1)
            coeff = w[:, j] * (own_inverse + inverse) - jnp.where(mate, 2.0, 0.0)
            dz += jnp.dot(coeff.astype(jnp.bfloat16), e[j, :], preferred_element_type=jnp.float32)
        start += e.shape[0]
    dz = dz * inv_temp
    unit, scale = normalized(own_ref[...])
    grad_ref[...] = scale * (dz - unit * jnp.sum(unit * dz, axis=-1, keepdims=True))


def whole_plan(feats, partner):
    rows, width = feats.shape
    stages = gather_rows(feats)
    mates = partner[None, :]
    f32, bf16 = jnp.float32, jnp.bfloat16
    vmem = pl.BlockSpec(memory_space=pltpu.VMEM)
    chunks, embeds, weights, sums, states = [], [], [], [], []
    done = 0
    for s, stage in enumerate(stages):
        if callable(stage):
            stage, sums = stage(sums)
        pieces = [piece for piece, _ in stage]
        chunks.append([chunk for _, part in stage for chunk in part])
        new = sum(piece.shape[0] for piece in pieces)
        state = [((new, width), bf16), ((rows, new), f32), ((8, done + new), f32)]
        final = s == len(stages) - 1
        outs = [((rows, width), f32), ((1, rows), f32)] if final else state + [((rows, rows), f32)]
        operands = [mates, feats, *embeds, *(weights if final else []), *sums, *pieces]
        results = pl.pallas_call(
            functools.partial(stage_kernel, list(chunks), final),
            out_shape=tuple(jax.ShapeDtypeStruct(shape, dtype) for shape, dtype in outs),
            in_specs=[vmem] * len(operands),
            out_specs=(vmem,) * len(outs),
            scratch_shapes=[pltpu.VMEM(shape, dtype) for shape, dtype in (state if final else [])],
            cost_estimate=pl.CostEstimate(flops=1000, bytes_accessed=0, transcendentals=0),
            compiler_params=pltpu.CompilerParams(vmem_limit_bytes=32 * 1024 * 1024),
        )(*operands)
        if not final:
            embeds.append(results[0])
            weights.append(results[1])
            sums = list(results[2:])
            states.append(sums)
        done += new
    grad, loss = results
    return grad, loss.reshape(rows)


def solution(mesh):
    every = mesh.shape["batch"] == 16 and mesh.shape["rep"] == 2
    in_specs = (P("batch", None), P("batch"))
    out_specs = (P("batch", None), P("batch"))
    return jax.shard_map(
        whole_plan if every else split_plan, mesh=mesh, in_specs=in_specs, out_specs=out_specs, check_vma=False
    )
```

```python
import functools
import math

import jax
import jax.numpy as jnp
from jax import lax
from jax.experimental import pallas as pl
from jax.experimental.pallas import tpu as pltpu
from jax.sharding import PartitionSpec as P

inv_temp = 10.0
log2e = 1.4426950408889634


def split_plan(feats, partner):
    rows, width = feats.shape
    layers = lax.axis_size("rep")
    share = rows // layers
    layer = lax.axis_index("rep")
    block_index = lax.axis_index("batch")
    hf = feats.astype(jnp.float32)
    scale = lax.rsqrt(jnp.sum(hf * hf, axis=-1, keepdims=True) + 1e-06)
    unit = hf * scale
    embed = unit.astype(jnp.bfloat16)
    own_ids = block_index * rows + jnp.arange(rows, dtype=jnp.int32)
    mine = lax.dynamic_slice_in_dim(embed, layer * share, share, 0)

    def key_ids(start, count):
        gathered = start + jnp.arange(count, dtype=jnp.int32)
        return gathered // share * rows + layer * share + gathered % share

    def first_fold(carry, piece, start):
        denom, pscore = carry
        score = jnp.dot(embed, piece.T, preferred_element_type=jnp.float32) * inv_temp
        ids = key_ids(start, piece.shape[0])
        weight = jnp.where(ids[None, :] == own_ids[:, None], 0.0, jnp.exp(score - inv_temp))
        hits = jnp.where(ids[None, :] == partner[:, None], score, 0.0)
        return (denom + jnp.sum(weight, axis=1), pscore + jnp.sum(hits, axis=1))

    empty_rows = jnp.zeros((rows,), jnp.float32)
    keys = lax.all_gather(mine, "batch", axis=0, tiled=True)
    group = math.gcd(lax.axis_size("batch"), max(1, 512 // share))
    span = group * share
    turns = keys.shape[0] // span
    stacked = keys.reshape(turns, span, width)
    starts = jnp.arange(turns, dtype=jnp.int32) * span

    def first_step(carry, item):
        return (first_fold(carry, item[0], item[1]), None)

    (denom, pscore), unused = lax.scan(first_step, (empty_rows, empty_rows), (stacked, starts))
    denom, pscore = lax.psum((denom, pscore), "rep")
    lse = jnp.log(denom) + inv_temp
    loss = lse - pscore
    lse_share = lax.dynamic_slice_in_dim(lse, layer * share, share, 0)

    def second_fold(acc, pieces, start):
        piece, piece_lse = pieces
        score = jnp.dot(embed, piece.T, preferred_element_type=jnp.float32) * inv_temp
        ids = key_ids(start, piece.shape[0])
        coeff = jnp.exp(score - lse[:, None]) + jnp.exp(score - piece_lse[None, :])
        coeff = coeff - 2.0 * jnp.where(ids[None, :] == partner[:, None], 1.0, 0.0)
        coeff = jnp.where(ids[None, :] == own_ids[:, None], 0.0, coeff).astype(jnp.bfloat16)
        return acc + jnp.dot(coeff, piece, preferred_element_type=jnp.float32)

    empty_acc = jnp.zeros((rows, width), jnp.float32)
    key_lse = lax.all_gather(lse_share, "batch", axis=0, tiled=True)
    stacked_lse = key_lse.reshape(turns, span)

    def second_step(acc, item):
        return (second_fold(acc, (item[0], item[1]), item[2]), None)

    acc, unused = lax.scan(second_step, empty_acc, (stacked, stacked_lse, starts))
    part_sum = lax.psum_scatter(acc, "rep", scatter_dimension=0, tiled=True)
    dz_share = part_sum * inv_temp
    unit_share = lax.dynamic_slice_in_dim(unit, layer * share, share, 0)
    scale_share = lax.dynamic_slice_in_dim(scale, layer * share, share, 0)
    grad_share = scale_share * (
        dz_share - unit_share * jnp.sum(unit_share * dz_share, axis=-1, keepdims=True)
    )
    grad = lax.all_gather(grad_share, "rep", axis=0, tiled=True)
    return (grad, loss)


X, Y, XY, Z1, Z2, Z3 = 1, 2, 3, 4, 8, 12


def send(piece, first, second=None):
    offsets = (first, first if second is None else second)
    pairs = [
        (2 * b + c, 2 * (b ^ offsets[c]) + c) for b in range(lax.axis_size("batch")) for c in range(2)
    ]
    return lax.ppermute(piece, ("batch", "rep"), pairs)


def swap(piece):
    return lax.ppermute(piece, "rep", [(0, 1), (1, 0)])


def join(*pieces):
    return jnp.concatenate(pieces, axis=0)


class Chunk:
    def __init__(self, offsets, parts=None):
        self.offsets = offsets
        self.parts = parts

    def swapped(self):
        return Chunk(self.offsets[::-1], self.parts and self.parts[::-1])


def halves(first, second, *within):
    return [Chunk((first ^ w, second ^ w), (0, 1)) for w in within]


def whole(first, second):
    return [Chunk((first, second))]


def gather_rows(feats):
    share = feats.shape[0] // 2
    layer = lax.axis_index("rep")

    def tie(value, *others):
        return lax.optimization_barrier((value, *others))

    def both(piece, chunks):
        return [(piece, chunks), (swap(piece), [chunk.swapped() for chunk in chunks])]

    far = send(feats, Z2, Z3)
    near = send(feats, X, Y)
    cross = send(feats, XY, Z1)
    far, near = tie(far, near)
    side_in = near
    side = send(side_in, Z1)
    far_x = send(far, X, Y)
    far_f = far
    far_xy = send(far_x, Y, X)
    far_y = send(far_f, Y, X)
    cross_in = cross
    side_xy = send(cross_in, Z1, XY)
    early = both(join(near, cross, far), whole(X, Y) + whole(XY, Z1) + whole(Z2, Z3))

    def last(sums):
        g, s, fy = far_xy, side, far_y
        sx = side_xy
        g, s, sx, hits = tie(far_xy, side, side_xy, sums[1])
        rest.extend(both(s, whole(X ^ Z1, Y ^ Z1)) + both(g, whole(XY ^ Z2, XY ^ Z3)) + [(sx, whole(XY ^ Z1, XY ^ Z1))])
        return both(join(far_x, fy), whole(X ^ Z2, Y ^ Z3) + whole(Y ^ Z2, X ^ Z3)), [sums[0], hits]

    rest = []
    return [[(feats, whole(0, 0))] + early, last, lambda sums: (rest, sums)]


def normalized(raw):
    hf = raw.astype(jnp.float32)
    scale = lax.rsqrt(jnp.sum(hf * hf, axis=-1, keepdims=True) + 1e-06)
    return hf * scale, scale


def normalize_into(embed, refs):
    start = 0
    for ref in refs:
        count = ref.shape[0]
        for at in range(0, count, 64):
            embed[start + at : start + at + 64, :] = normalized(ref[at : at + 64, :])[0].astype(jnp.bfloat16)
        start += count


def partner_column(partner_ref):
    rows = partner_ref.shape[1]
    spread = jnp.broadcast_to(partner_ref[...], (rows, rows)).astype(jnp.float32)
    return jnp.sum(jnp.where(diagonal(rows), spread, 0.0), axis=1, keepdims=True).astype(jnp.int32)


def diagonal(size):
    r = lax.broadcasted_iota(jnp.int32, (size, size), 0)
    c = lax.broadcasted_iota(jnp.int32, (size, size), 1)
    return r == c


def column_ids(chunks, rows):
    layer = lax.axis_index("rep")
    block = lax.axis_index("batch")
    lane = lax.broadcasted_iota(jnp.int32, (1, rows), 1)
    share = rows // 2

    def base(chunk):
        first = (block ^ jnp.where(layer == 0, *chunk.offsets)) * rows
        return first if chunk.parts is None else first + jnp.where(layer == 0, *chunk.parts) * share

    groups = {}
    start = 0
    for chunk in chunks:
        stop = start + (rows if chunk.parts is None else share)
        for group in range(start // rows, (stop - 1) // rows + 1):
            value = lane + (base(chunk) + group * rows - start)
            before = groups.get(group)
            groups[group] = value if before is None else jnp.where(lane < start - group * rows, before, value)
        start = stop
    return [groups[group] for group in range(start // rows)]


def spans(total, block):
    return [slice(start, min(start + block, total)) for start in range(0, total, block)]


def shift(span, by):
    return slice(span.start + by, span.stop + by)


def weigh(left, right):
    score = lax.dot_general(left, right, (((1,), (1,)), ((), ())), preferred_element_type=jnp.float32)
    return score, jnp.exp2(score * (inv_temp * log2e))


def fold_rows(weight):
    return jnp.sum(weight.reshape(weight.shape[0] // 8, 8, weight.shape[1]), axis=0)


def fold_columns(weight):
    return sum(weight[:, k : k + 128] for k in range(0, weight.shape[1], 128))


def triangle(embed, total, block, denom, top):
    blocks = total // block
    for i in range(blocks):
        left = embed[i * block : (i + 1) * block, :]
        row_sum = jnp.zeros((block, 128), jnp.float32)
        for j in range(i, blocks):
            score, weight = weigh(left, embed[j * block : (j + 1) * block, :])
            if i == j:
                weight = jnp.where(diagonal(block), 0.0, weight)
            else:
                row_sum += fold_columns(weight)
            if i == 0:
                top(j, score, weight)
            denom[:, j * block : (j + 1) * block] += fold_rows(weight)
        if i != blocks - 1:
            denom[:, i * block : (i + 1) * block] += fold_rows(row_sum.T)


def stage_kernel(chunks, final, partner_ref, own_ref, *refs):
    before = chunks[:-1]
    refs = list(refs)

    def take(count):
        taken = refs[:count]
        del refs[:count]
        return taken

    old_embeds = take(len(before))
    old_weights = take(len(before)) if final else []
    old_denom, old_hits = take(2) if before else (None, None)
    if final:
        grad_ref, loss_ref, embed, weights, denom = refs[-5:]
        pieces = refs[:-5]
    else:
        embed, weights, denom, hits_ref = refs[-4:]
        pieces = refs[:-4]
    rows, width = own_ref.shape
    block = 2 * rows
    new = embed.shape[0]
    old = denom.shape[1] - new

    normalize_into(embed, pieces)
    mates = partner_column(partner_ref)
    ids = [column_ids(part, rows) for part in chunks]
    hits = old_hits[...] if before else jnp.zeros((rows, rows), jnp.float32)
    if before:
        denom[:, :old] = old_denom[...]
    denom[:, old:] = jnp.zeros((8, new), jnp.float32)

    def is_mate(names, span):
        return [name == mates for name in names[span.start // rows : span.stop // rows]]

    def found(span, score):
        return sum(
            jnp.where(mate, score[:rows, k * rows : (k + 1) * rows], 0.0)
            for k, mate in enumerate(is_mate(ids[-1], span))
        )

    start = 0
    for old_embed in old_embeds:
        for i in spans(old_embed.shape[0], 2 * block):
            left = old_embed[i, :]
            row_sum = jnp.zeros((left.shape[0], 128), jnp.float32)
            for j in spans(new, block):
                score, weight = weigh(left, embed[j, :])
                if start + i.start == 0:
                    weights[:, j] = weight[:rows]
                    hits += found(j, score)
                row_sum += fold_columns(weight)
                denom[:, shift(j, old)] += fold_rows(weight)
            denom[:, shift(i, start)] += fold_rows(row_sum.T)
        start += old_embed.shape[0]
    for i in spans(new, block):
        left = embed[i, :]
        row_sum = jnp.zeros((left.shape[0], 128), jnp.float32)
        for j in spans(new, block):
            if j.start < i.start:
                continue
            score, weight = weigh(left, embed[j, :])
            if i == j:
                weight = jnp.where(diagonal(weight.shape[0]), 0.0, weight)
            else:
                row_sum += fold_columns(weight)
            if not before and i.start == 0:
                weights[:, j] = weight[:rows]
                hits += found(j, score)
            denom[:, shift(j, old)] += fold_rows(weight)
        if i.stop != new:
            denom[:, shift(i, old)] += fold_rows(row_sum.T)
    if not final:
        hits_ref[...] = hits
        return

    all_weights = [*old_weights, weights]
    own = jnp.sum(sum(fold_columns(w[...]) for w in all_weights), axis=1, keepdims=True)
    loss = jnp.log(own) - inv_temp * jnp.sum(hits, axis=1, keepdims=True)
    loss_ref[...] = jnp.sum(jnp.where(diagonal(rows), loss, 0.0), axis=0, keepdims=True)
    own_inverse = 1.0 / own
    dz = jnp.zeros((rows, width), jnp.float32)
    start = 0
    for e, w, names in zip([*old_embeds, embed], all_weights, ids):
        for j in spans(e.shape[0], block):
            inverse = 1.0 / jnp.sum(denom[:, shift(j, start)], axis=0, keepdims=True)
            mate = jnp.concatenate(is_mate(names, j), axis=1)
            coeff = w[:, j] * (own_inverse + inverse) - jnp.where(mate, 2.0, 0.0)
            dz += jnp.dot(coeff.astype(jnp.bfloat16), e[j, :], preferred_element_type=jnp.float32)
        start += e.shape[0]
    dz = dz * inv_temp
    unit, scale = normalized(own_ref[...])
    grad_ref[...] = scale * (dz - unit * jnp.sum(unit * dz, axis=-1, keepdims=True))


def whole_plan(feats, partner):
    rows, width = feats.shape
    stages = gather_rows(feats)
    mates = partner[None, :]
    f32, bf16 = jnp.float32, jnp.bfloat16
    vmem = pl.BlockSpec(memory_space=pltpu.VMEM)
    chunks, embeds, weights, sums, states = [], [], [], [], []
    done = 0
    for s, stage in enumerate(stages):
        if callable(stage):
            stage, sums = stage(sums)
        pieces = [piece for piece, _ in stage]
        chunks.append([chunk for _, part in stage for chunk in part])
        new = sum(piece.shape[0] for piece in pieces)
        state = [((new, width), bf16), ((rows, new), f32), ((8, done + new), f32)]
        final = s == len(stages) - 1
        outs = [((rows, width), f32), ((1, rows), f32)] if final else state + [((rows, rows), f32)]
        operands = [mates, feats, *embeds, *(weights if final else []), *sums, *pieces]
        results = pl.pallas_call(
            functools.partial(stage_kernel, list(chunks), final),
            out_shape=tuple(jax.ShapeDtypeStruct(shape, dtype) for shape, dtype in outs),
            in_specs=[vmem] * len(operands),
            out_specs=(vmem,) * len(outs),
            scratch_shapes=[pltpu.VMEM(shape, dtype) for shape, dtype in (state if final else [])],
            cost_estimate=pl.CostEstimate(flops=1000, bytes_accessed=0, transcendentals=0),
            compiler_params=pltpu.CompilerParams(vmem_limit_bytes=32 * 1024 * 1024),
        )(*operands)
        if not final:
            embeds.append(results[0])
            weights.append(results[1])
            sums = list(results[2:])
            states.append(sums)
        done += new
    grad, loss = results
    return grad, loss.reshape(rows)


def solution(mesh):
    every = mesh.shape["batch"] == 16 and mesh.shape["rep"] == 2
    in_specs = (P("batch", None), P("batch"))
    out_specs = (P("batch", None), P("batch"))
    return jax.shard_map(
        whole_plan if every else split_plan, mesh=mesh, in_specs=in_specs, out_specs=out_specs, check_vma=False
    )
```

```python
import functools
import math

import jax
import jax.numpy as jnp
from jax import lax
from jax.experimental import pallas as pl
from jax.experimental.pallas import tpu as pltpu
from jax.sharding import PartitionSpec as P

inv_temp = 10.0
log2e = 1.4426950408889634


def split_plan(feats, partner):
    rows, width = feats.shape
    layers = lax.axis_size("rep")
    share = rows // layers
    layer = lax.axis_index("rep")
    block_index = lax.axis_index("batch")
    hf = feats.astype(jnp.float32)
    scale = lax.rsqrt(jnp.sum(hf * hf, axis=-1, keepdims=True) + 1e-06)
    unit = hf * scale
    embed = unit.astype(jnp.bfloat16)
    own_ids = block_index * rows + jnp.arange(rows, dtype=jnp.int32)
    mine = lax.dynamic_slice_in_dim(embed, layer * share, share, 0)

    def key_ids(start, count):
        gathered = start + jnp.arange(count, dtype=jnp.int32)
        return gathered // share * rows + layer * share + gathered % share

    def first_fold(carry, piece, start):
        denom, pscore = carry
        score = jnp.dot(embed, piece.T, preferred_element_type=jnp.float32) * inv_temp
        ids = key_ids(start, piece.shape[0])
        weight = jnp.where(ids[None, :] == own_ids[:, None], 0.0, jnp.exp(score - inv_temp))
        hits = jnp.where(ids[None, :] == partner[:, None], score, 0.0)
        return (denom + jnp.sum(weight, axis=1), pscore + jnp.sum(hits, axis=1))

    empty_rows = jnp.zeros((rows,), jnp.float32)
    keys = lax.all_gather(mine, "batch", axis=0, tiled=True)
    group = math.gcd(lax.axis_size("batch"), max(1, 512 // share))
    span = group * share
    turns = keys.shape[0] // span
    stacked = keys.reshape(turns, span, width)
    starts = jnp.arange(turns, dtype=jnp.int32) * span

    def first_step(carry, item):
        return (first_fold(carry, item[0], item[1]), None)

    (denom, pscore), unused = lax.scan(first_step, (empty_rows, empty_rows), (stacked, starts))
    denom, pscore = lax.psum((denom, pscore), "rep")
    lse = jnp.log(denom) + inv_temp
    loss = lse - pscore
    lse_share = lax.dynamic_slice_in_dim(lse, layer * share, share, 0)

    def second_fold(acc, pieces, start):
        piece, piece_lse = pieces
        score = jnp.dot(embed, piece.T, preferred_element_type=jnp.float32) * inv_temp
        ids = key_ids(start, piece.shape[0])
        coeff = jnp.exp(score - lse[:, None]) + jnp.exp(score - piece_lse[None, :])
        coeff = coeff - 2.0 * jnp.where(ids[None, :] == partner[:, None], 1.0, 0.0)
        coeff = jnp.where(ids[None, :] == own_ids[:, None], 0.0, coeff).astype(jnp.bfloat16)
        return acc + jnp.dot(coeff, piece, preferred_element_type=jnp.float32)

    empty_acc = jnp.zeros((rows, width), jnp.float32)
    key_lse = lax.all_gather(lse_share, "batch", axis=0, tiled=True)
    stacked_lse = key_lse.reshape(turns, span)

    def second_step(acc, item):
        return (second_fold(acc, (item[0], item[1]), item[2]), None)

    acc, unused = lax.scan(second_step, empty_acc, (stacked, stacked_lse, starts))
    part_sum = lax.psum_scatter(acc, "rep", scatter_dimension=0, tiled=True)
    dz_share = part_sum * inv_temp
    unit_share = lax.dynamic_slice_in_dim(unit, layer * share, share, 0)
    scale_share = lax.dynamic_slice_in_dim(scale, layer * share, share, 0)
    grad_share = scale_share * (
        dz_share - unit_share * jnp.sum(unit_share * dz_share, axis=-1, keepdims=True)
    )
    grad = lax.all_gather(grad_share, "rep", axis=0, tiled=True)
    return (grad, loss)


X, Y, XY, Z1, Z2, Z3 = 1, 2, 3, 4, 8, 12


def send(piece, first, second=None):
    offsets = (first, first if second is None else second)
    pairs = [
        (2 * b + c, 2 * (b ^ offsets[c]) + c) for b in range(lax.axis_size("batch")) for c in range(2)
    ]
    return lax.ppermute(piece, ("batch", "rep"), pairs)


def swap(piece):
    return lax.ppermute(piece, "rep", [(0, 1), (1, 0)])


def join(*pieces):
    return jnp.concatenate(pieces, axis=0)


class Chunk:
    def __init__(self, offsets, parts=None):
        self.offsets = offsets
        self.parts = parts

    def swapped(self):
        return Chunk(self.offsets[::-1], self.parts and self.parts[::-1])


def halves(first, second, *within):
    return [Chunk((first ^ w, second ^ w), (0, 1)) for w in within]


def whole(first, second):
    return [Chunk((first, second))]


def gather_rows(feats):
    far = send(feats, Z2, Z3)
    near = send(feats, X, Y)
    cross = send(feats, XY, Z1)
    side = send(near, Z1)
    side_xy = send(cross, Z1, XY)
    far_x, far_y = send(far, X, Y), send(far, Y, X)
    far_xy = send(far_x, Y, X)
    held = {}

    def tie(value, *others):
        return lax.optimization_barrier((value, *others))

    def both(piece, chunks):
        return [(piece, chunks), (swap(piece), [chunk.swapped() for chunk in chunks])]

    NC, CC, FC = whole(X, Y), whole(XY, Z1), whole(Z2, Z3)
    EC = whole(X ^ Z2, Y ^ Z3)
    YC = whole(Y ^ Z2, X ^ Z3)
    GC = whole(XY ^ Z2, XY ^ Z3)
    SC = whole(X ^ Z1, Y ^ Z1)
    SX = whole(XY ^ Z1, XY ^ Z1)

    def other(piece, chunks):
        return both(piece, chunks)[1]

    pair = join(far_x, far_y)
    early = both(join(near, cross, far), NC + CC + FC) + [(pair, EC + YC)]

    def second(sums):
        s, sx, g, hits = side, side_xy, far_xy, sums[1]
        s, sx, hits = tie(s, sx, hits)
        held.update(s=s, sx=sx, g=g)
        return [(s, SC), (sx, SX)], [sums[0], hits]

    def third(sums):
        s, sx, g, hits = held["s"], held["sx"], held["g"], sums[1]
        g, s, hits = tie(g, s, hits)
        held.update(s=s, sx=sx, g=g)
        return [other(pair, EC + YC)], [sums[0], hits]

    def last(sums):
        s, sx, g = held["s"], held["sx"], held["g"]
        return both(g, GC) + [other(s, SC)], sums

    return [[(feats, whole(0, 0))] + early, second, third, last]


def normalized(raw):
    hf = raw.astype(jnp.float32)
    scale = lax.rsqrt(jnp.sum(hf * hf, axis=-1, keepdims=True) + 1e-06)
    return hf * scale, scale


def normalize_into(embed, refs):
    start = 0
    for ref in refs:
        count = ref.shape[0]
        for at in range(0, count, 64):
            embed[start + at : start + at + 64, :] = normalized(ref[at : at + 64, :])[0].astype(jnp.bfloat16)
        start += count


def partner_column(partner_ref):
    rows = partner_ref.shape[1]
    spread = jnp.broadcast_to(partner_ref[...], (rows, rows)).astype(jnp.float32)
    return jnp.sum(jnp.where(diagonal(rows), spread, 0.0), axis=1, keepdims=True).astype(jnp.int32)


def diagonal(size):
    r = lax.broadcasted_iota(jnp.int32, (size, size), 0)
    c = lax.broadcasted_iota(jnp.int32, (size, size), 1)
    return r == c


def column_ids(chunks, rows):
    layer = lax.axis_index("rep")
    block = lax.axis_index("batch")
    lane = lax.broadcasted_iota(jnp.int32, (1, rows), 1)
    share = rows // 2

    def base(chunk):
        first = (block ^ jnp.where(layer == 0, *chunk.offsets)) * rows
        return first if chunk.parts is None else first + jnp.where(layer == 0, *chunk.parts) * share

    groups = {}
    start = 0
    for chunk in chunks:
        stop = start + (rows if chunk.parts is None else share)
        for group in range(start // rows, (stop - 1) // rows + 1):
            value = lane + (base(chunk) + group * rows - start)
            before = groups.get(group)
            groups[group] = value if before is None else jnp.where(lane < start - group * rows, before, value)
        start = stop
    return [groups[group] for group in range(start // rows)]


def spans(total, block):
    return [slice(start, min(start + block, total)) for start in range(0, total, block)]


def shift(span, by):
    return slice(span.start + by, span.stop + by)


def weigh(left, right):
    score = lax.dot_general(left, right, (((1,), (1,)), ((), ())), preferred_element_type=jnp.float32)
    return score, jnp.exp2(score * (inv_temp * log2e))


def fold_rows(weight):
    return jnp.sum(weight.reshape(weight.shape[0] // 8, 8, weight.shape[1]), axis=0)


def fold_columns(weight):
    return sum(weight[:, k : k + 128] for k in range(0, weight.shape[1], 128))


def triangle(embed, total, block, denom, top):
    blocks = total // block
    for i in range(blocks):
        left = embed[i * block : (i + 1) * block, :]
        row_sum = jnp.zeros((block, 128), jnp.float32)
        for j in range(i, blocks):
            score, weight = weigh(left, embed[j * block : (j + 1) * block, :])
            if i == j:
                weight = jnp.where(diagonal(block), 0.0, weight)
            else:
                row_sum += fold_columns(weight)
            if i == 0:
                top(j, score, weight)
            denom[:, j * block : (j + 1) * block] += fold_rows(weight)
        if i != blocks - 1:
            denom[:, i * block : (i + 1) * block] += fold_rows(row_sum.T)


def stage_kernel(chunks, final, partner_ref, own_ref, *refs):
    before = chunks[:-1]
    refs = list(refs)

    def take(count):
        taken = refs[:count]
        del refs[:count]
        return taken

    old_embeds = take(len(before))
    old_weights = take(len(before)) if final else []
    old_denom, old_hits = take(2) if before else (None, None)
    if final:
        grad_ref, loss_ref, embed, weights, denom = refs[-5:]
        pieces = refs[:-5]
    else:
        embed, weights, denom, hits_ref = refs[-4:]
        pieces = refs[:-4]
    rows, width = own_ref.shape
    block = 2 * rows
    new = embed.shape[0]
    old = denom.shape[1] - new

    normalize_into(embed, pieces)
    mates = partner_column(partner_ref)
    ids = [column_ids(part, rows) for part in chunks]
    hits = old_hits[...] if before else jnp.zeros((rows, rows), jnp.float32)
    if before:
        denom[:, :old] = old_denom[...]
    denom[:, old:] = jnp.zeros((8, new), jnp.float32)

    def is_mate(names, span):
        return [name == mates for name in names[span.start // rows : span.stop // rows]]

    def found(span, score):
        return sum(
            jnp.where(mate, score[:rows, k * rows : (k + 1) * rows], 0.0)
            for k, mate in enumerate(is_mate(ids[-1], span))
        )

    start = 0
    for old_embed in old_embeds:
        for i in spans(old_embed.shape[0], 2 * block):
            left = old_embed[i, :]
            row_sum = jnp.zeros((left.shape[0], 128), jnp.float32)
            for j in spans(new, block):
                score, weight = weigh(left, embed[j, :])
                if start + i.start == 0:
                    weights[:, j] = weight[:rows]
                    hits += found(j, score)
                row_sum += fold_columns(weight)
                denom[:, shift(j, old)] += fold_rows(weight)
            denom[:, shift(i, start)] += fold_rows(row_sum.T)
        start += old_embed.shape[0]
    small = rows if final and new <= 3 * rows else block
    for i in spans(new, small):
        left = embed[i, :]
        row_sum = jnp.zeros((left.shape[0], 128), jnp.float32)
        for j in spans(new, small):
            if j.start < i.start:
                continue
            score, weight = weigh(left, embed[j, :])
            if i == j:
                weight = jnp.where(diagonal(weight.shape[0]), 0.0, weight)
            else:
                row_sum += fold_columns(weight)
            if not before and i.start == 0:
                weights[:, j] = weight[:rows]
                hits += found(j, score)
            denom[:, shift(j, old)] += fold_rows(weight)
        if i.stop != new:
            denom[:, shift(i, old)] += fold_rows(row_sum.T)
    if not final:
        hits_ref[...] = hits
        return

    all_weights = [*old_weights, weights]
    own = jnp.sum(sum(fold_columns(w[...]) for w in all_weights), axis=1, keepdims=True)
    loss = jnp.log(own) - inv_temp * jnp.sum(hits, axis=1, keepdims=True)
    loss_ref[...] = jnp.sum(jnp.where(diagonal(rows), loss, 0.0), axis=0, keepdims=True)
    own_inverse = 1.0 / own
    dz = jnp.zeros((rows, width), jnp.float32)
    start = 0
    for e, w, names in zip([*old_embeds, embed], all_weights, ids):
        for j in spans(e.shape[0], block):
            inverse = 1.0 / jnp.sum(denom[:, shift(j, start)], axis=0, keepdims=True)
            mate = jnp.concatenate(is_mate(names, j), axis=1)
            coeff = w[:, j] * (own_inverse + inverse) - jnp.where(mate, 2.0, 0.0)
            dz += jnp.dot(coeff.astype(jnp.bfloat16), e[j, :], preferred_element_type=jnp.float32)
        start += e.shape[0]
    dz = dz * inv_temp
    unit, scale = normalized(own_ref[...])
    grad_ref[...] = scale * (dz - unit * jnp.sum(unit * dz, axis=-1, keepdims=True))


def whole_plan(feats, partner):
    rows, width = feats.shape
    stages = gather_rows(feats)
    mates = partner[None, :]
    f32, bf16 = jnp.float32, jnp.bfloat16
    vmem = pl.BlockSpec(memory_space=pltpu.VMEM)
    chunks, embeds, weights, sums, states = [], [], [], [], []
    done = 0
    for s, stage in enumerate(stages):
        if callable(stage):
            stage, sums = stage(sums)
        pieces = [piece for piece, _ in stage]
        chunks.append([chunk for _, part in stage for chunk in part])
        new = sum(piece.shape[0] for piece in pieces)
        state = [((new, width), bf16), ((rows, new), f32), ((8, done + new), f32)]
        final = s == len(stages) - 1
        outs = [((rows, width), f32), ((1, rows), f32)] if final else state + [((rows, rows), f32)]
        operands = [mates, feats, *embeds, *(weights if final else []), *sums, *pieces]
        results = pl.pallas_call(
            functools.partial(stage_kernel, list(chunks), final),
            out_shape=tuple(jax.ShapeDtypeStruct(shape, dtype) for shape, dtype in outs),
            in_specs=[vmem] * len(operands),
            out_specs=(vmem,) * len(outs),
            scratch_shapes=[pltpu.VMEM(shape, dtype) for shape, dtype in (state if final else [])],
            cost_estimate=pl.CostEstimate(flops=1000, bytes_accessed=0, transcendentals=0),
            compiler_params=pltpu.CompilerParams(vmem_limit_bytes=32 * 1024 * 1024),
        )(*operands)
        if not final:
            embeds.append(results[0])
            weights.append(results[1])
            sums = list(results[2:])
            states.append(sums)
        done += new
    grad, loss = results
    return grad, loss.reshape(rows)


def solution(mesh):
    every = mesh.shape["batch"] == 16 and mesh.shape["rep"] == 2
    in_specs = (P("batch", None), P("batch"))
    out_specs = (P("batch", None), P("batch"))
    return jax.shard_map(
        whole_plan if every else split_plan, mesh=mesh, in_specs=in_specs, out_specs=out_specs, check_vma=False
    )
```

```python
import functools
import math

import jax
import jax.numpy as jnp
from jax import lax
from jax.experimental import pallas as pl
from jax.experimental.pallas import tpu as pltpu
from jax.sharding import PartitionSpec as P

inv_temp = 10.0
log2e = 1.4426950408889634


def split_plan(feats, partner):
    rows, width = feats.shape
    layers = lax.axis_size("rep")
    share = rows // layers
    layer = lax.axis_index("rep")
    block_index = lax.axis_index("batch")
    hf = feats.astype(jnp.float32)
    scale = lax.rsqrt(jnp.sum(hf * hf, axis=-1, keepdims=True) + 1e-06)
    unit = hf * scale
    embed = unit.astype(jnp.bfloat16)
    own_ids = block_index * rows + jnp.arange(rows, dtype=jnp.int32)
    mine = lax.dynamic_slice_in_dim(embed, layer * share, share, 0)

    def key_ids(start, count):
        gathered = start + jnp.arange(count, dtype=jnp.int32)
        return gathered // share * rows + layer * share + gathered % share

    def first_fold(carry, piece, start):
        denom, pscore = carry
        score = jnp.dot(embed, piece.T, preferred_element_type=jnp.float32) * inv_temp
        ids = key_ids(start, piece.shape[0])
        weight = jnp.where(ids[None, :] == own_ids[:, None], 0.0, jnp.exp(score - inv_temp))
        hits = jnp.where(ids[None, :] == partner[:, None], score, 0.0)
        return (denom + jnp.sum(weight, axis=1), pscore + jnp.sum(hits, axis=1))

    empty_rows = jnp.zeros((rows,), jnp.float32)
    keys = lax.all_gather(mine, "batch", axis=0, tiled=True)
    group = math.gcd(lax.axis_size("batch"), max(1, 512 // share))
    span = group * share
    turns = keys.shape[0] // span
    stacked = keys.reshape(turns, span, width)
    starts = jnp.arange(turns, dtype=jnp.int32) * span

    def first_step(carry, item):
        return (first_fold(carry, item[0], item[1]), None)

    (denom, pscore), unused = lax.scan(first_step, (empty_rows, empty_rows), (stacked, starts))
    denom, pscore = lax.psum((denom, pscore), "rep")
    lse = jnp.log(denom) + inv_temp
    loss = lse - pscore
    lse_share = lax.dynamic_slice_in_dim(lse, layer * share, share, 0)

    def second_fold(acc, pieces, start):
        piece, piece_lse = pieces
        score = jnp.dot(embed, piece.T, preferred_element_type=jnp.float32) * inv_temp
        ids = key_ids(start, piece.shape[0])
        coeff = jnp.exp(score - lse[:, None]) + jnp.exp(score - piece_lse[None, :])
        coeff = coeff - 2.0 * jnp.where(ids[None, :] == partner[:, None], 1.0, 0.0)
        coeff = jnp.where(ids[None, :] == own_ids[:, None], 0.0, coeff).astype(jnp.bfloat16)
        return acc + jnp.dot(coeff, piece, preferred_element_type=jnp.float32)

    empty_acc = jnp.zeros((rows, width), jnp.float32)
    key_lse = lax.all_gather(lse_share, "batch", axis=0, tiled=True)
    stacked_lse = key_lse.reshape(turns, span)

    def second_step(acc, item):
        return (second_fold(acc, (item[0], item[1]), item[2]), None)

    acc, unused = lax.scan(second_step, empty_acc, (stacked, stacked_lse, starts))
    part_sum = lax.psum_scatter(acc, "rep", scatter_dimension=0, tiled=True)
    dz_share = part_sum * inv_temp
    unit_share = lax.dynamic_slice_in_dim(unit, layer * share, share, 0)
    scale_share = lax.dynamic_slice_in_dim(scale, layer * share, share, 0)
    grad_share = scale_share * (
        dz_share - unit_share * jnp.sum(unit_share * dz_share, axis=-1, keepdims=True)
    )
    grad = lax.all_gather(grad_share, "rep", axis=0, tiled=True)
    return (grad, loss)


X, Y, XY, Z1, Z2, Z3 = 1, 2, 3, 4, 8, 12


def send(piece, first, second=None):
    offsets = (first, first if second is None else second)
    pairs = [
        (2 * b + c, 2 * (b ^ offsets[c]) + c) for b in range(lax.axis_size("batch")) for c in range(2)
    ]
    return lax.ppermute(piece, ("batch", "rep"), pairs)


def swap(piece):
    return lax.ppermute(piece, "rep", [(0, 1), (1, 0)])


def join(*pieces):
    return jnp.concatenate(pieces, axis=0)


class Chunk:
    def __init__(self, *offsets):
        self.offsets = offsets

    def swapped(self):
        return Chunk(*self.offsets[::-1])


def tie(*values):
    return lax.optimization_barrier(values)


def gather_rows(feats):
    far = send(feats, Z2, Z3)
    near = send(feats, X, Y)
    cross = send(feats, XY, Z1)
    far, near = tie(far, near)
    side = send(near, Z1)
    side_xy = send(cross, Z1, XY)
    far_x, far_y = send(far, X, Y), send(far, Y, X)
    far_xy = send(far_x, Y, X)
    early = join(near, cross, far)
    pair = join(far_x, far_y)
    early_chunks = [Chunk(X, Y), Chunk(XY, Z1), Chunk(Z2, Z3)]
    pair_chunks = [Chunk(X ^ Z2, Y ^ Z3), Chunk(Y ^ Z2, X ^ Z3)]
    far_xy_chunks = [Chunk(XY ^ Z2, XY ^ Z3)]
    side_chunks = [Chunk(X ^ Z1, Y ^ Z1)]
    held = {}

    def other(piece, chunks):
        return swap(piece), [chunk.swapped() for chunk in chunks]

    def first(sums):
        return [(feats, [Chunk(0, 0)]), (early, early_chunks), other(early, early_chunks), (pair, pair_chunks)], sums

    def second(sums):
        held["side"], piece, hits = tie(side, side_xy, sums[1])
        return [(held["side"], side_chunks), (piece, [Chunk(XY ^ Z1, XY ^ Z1)])], [sums[0], hits]

    def third(sums):
        held["far_xy"], held["side"], hits = tie(far_xy, held["side"], sums[1])
        return [(held["far_xy"], far_xy_chunks), other(pair, pair_chunks)], [sums[0], hits]

    def last(sums):
        piece = held["far_xy"]
        return [other(piece, far_xy_chunks), other(held["side"], side_chunks)], sums

    return [first, second, third, last]


def normalized(raw):
    hf = raw.astype(jnp.float32)
    scale = lax.rsqrt(jnp.sum(hf * hf, axis=-1, keepdims=True) + 1e-06)
    return hf * scale, scale


def normalize_into(embed, refs):
    start = 0
    for ref in refs:
        count = ref.shape[0]
        for at in range(0, count, 64):
            embed[start + at : start + at + 64, :] = normalized(ref[at : at + 64, :])[0].astype(jnp.bfloat16)
        start += count


def partner_column(partner_ref):
    rows = partner_ref.shape[1]
    spread = jnp.broadcast_to(partner_ref[...], (rows, rows)).astype(jnp.float32)
    return jnp.sum(jnp.where(diagonal(rows), spread, 0.0), axis=1, keepdims=True).astype(jnp.int32)


def diagonal(size):
    r = lax.broadcasted_iota(jnp.int32, (size, size), 0)
    c = lax.broadcasted_iota(jnp.int32, (size, size), 1)
    return r == c


def column_ids(chunks, rows):
    layer = lax.axis_index("rep")
    block = lax.axis_index("batch")
    lane = lax.broadcasted_iota(jnp.int32, (1, rows), 1)
    return [lane + (block ^ jnp.where(layer == 0, *chunk.offsets)) * rows for chunk in chunks]


def spans(total, block):
    return [slice(start, min(start + block, total)) for start in range(0, total, block)]


def shift(span, by):
    return slice(span.start + by, span.stop + by)


def weigh(left, right):
    score = lax.dot_general(left, right, (((1,), (1,)), ((), ())), preferred_element_type=jnp.float32)
    return score, jnp.exp2(score * (inv_temp * log2e))


def fold_rows(weight):
    return jnp.sum(weight.reshape(weight.shape[0] // 8, 8, weight.shape[1]), axis=0)


def fold_columns(weight):
    return sum(weight[:, k : k + 128] for k in range(0, weight.shape[1], 128))


def triangle(embed, total, block, denom, top):
    blocks = total // block
    for i in range(blocks):
        left = embed[i * block : (i + 1) * block, :]
        row_sum = jnp.zeros((block, 128), jnp.float32)
        for j in range(i, blocks):
            score, weight = weigh(left, embed[j * block : (j + 1) * block, :])
            if i == j:
                weight = jnp.where(diagonal(block), 0.0, weight)
            else:
                row_sum += fold_columns(weight)
            if i == 0:
                top(j, score, weight)
            denom[:, j * block : (j + 1) * block] += fold_rows(weight)
        if i != blocks - 1:
            denom[:, i * block : (i + 1) * block] += fold_rows(row_sum.T)


def stage_kernel(chunks, final, partner_ref, own_ref, *refs):
    before = chunks[:-1]
    refs = list(refs)

    def take(count):
        taken = refs[:count]
        del refs[:count]
        return taken

    old_embeds = take(len(before))
    old_weights = take(len(before)) if final else []
    old_denom, old_hits = take(2) if before else (None, None)
    if final:
        grad_ref, loss_ref, embed, weights, denom = refs[-5:]
        pieces = refs[:-5]
    else:
        embed, weights, denom, hits_ref = refs[-4:]
        pieces = refs[:-4]
    rows, width = own_ref.shape
    block = 2 * rows
    new = embed.shape[0]
    old = denom.shape[1] - new

    normalize_into(embed, pieces)
    mates = partner_column(partner_ref)
    ids = [column_ids(part, rows) for part in chunks]
    hits = old_hits[...] if before else jnp.zeros((rows, rows), jnp.float32)
    if before:
        denom[:, :old] = old_denom[...]
    denom[:, old:] = jnp.zeros((8, new), jnp.float32)

    def is_mate(names, span):
        return [name == mates for name in names[span.start // rows : span.stop // rows]]

    def found(span, score):
        return sum(
            jnp.where(mate, score[:rows, k * rows : (k + 1) * rows], 0.0)
            for k, mate in enumerate(is_mate(ids[-1], span))
        )

    start = 0
    for old_embed in old_embeds:
        for i in spans(old_embed.shape[0], 2 * block):
            left = old_embed[i, :]
            row_sum = jnp.zeros((left.shape[0], 128), jnp.float32)
            for j in spans(new, block):
                score, weight = weigh(left, embed[j, :])
                if start + i.start == 0:
                    weights[:, j] = weight[:rows]
                    hits += found(j, score)
                row_sum += fold_columns(weight)
                denom[:, shift(j, old)] += fold_rows(weight)
            denom[:, shift(i, start)] += fold_rows(row_sum.T)
        start += old_embed.shape[0]
    small = rows if final and new <= 3 * rows else block
    for i in spans(new, small):
        left = embed[i, :]
        row_sum = jnp.zeros((left.shape[0], 128), jnp.float32)
        for j in spans(new, small):
            if j.start < i.start:
                continue
            score, weight = weigh(left, embed[j, :])
            if i == j:
                weight = jnp.where(diagonal(weight.shape[0]), 0.0, weight)
            else:
                row_sum += fold_columns(weight)
            if not before and i.start == 0:
                weights[:, j] = weight[:rows]
                hits += found(j, score)
            denom[:, shift(j, old)] += fold_rows(weight)
        if i.stop != new:
            denom[:, shift(i, old)] += fold_rows(row_sum.T)
    if not final:
        hits_ref[...] = hits
        return

    all_weights = [*old_weights, weights]
    own = jnp.sum(sum(fold_columns(w[...]) for w in all_weights), axis=1, keepdims=True)
    loss = jnp.log(own) - inv_temp * jnp.sum(hits, axis=1, keepdims=True)
    loss_ref[...] = jnp.sum(jnp.where(diagonal(rows), loss, 0.0), axis=0, keepdims=True)
    own_inverse = 1.0 / own
    dz = jnp.zeros((rows, width), jnp.float32)
    start = 0
    for e, w, names in zip([*old_embeds, embed], all_weights, ids):
        for j in spans(e.shape[0], block):
            inverse = 1.0 / jnp.sum(denom[:, shift(j, start)], axis=0, keepdims=True)
            mate = jnp.concatenate(is_mate(names, j), axis=1)
            coeff = w[:, j] * (own_inverse + inverse) - jnp.where(mate, 2.0, 0.0)
            dz += jnp.dot(coeff.astype(jnp.bfloat16), e[j, :], preferred_element_type=jnp.float32)
        start += e.shape[0]
    dz = dz * inv_temp
    unit, scale = normalized(own_ref[...])
    grad_ref[...] = scale * (dz - unit * jnp.sum(unit * dz, axis=-1, keepdims=True))


def whole_plan(feats, partner):
    rows, width = feats.shape
    mates = partner[None, :]
    f32, bf16 = jnp.float32, jnp.bfloat16
    vmem = pl.BlockSpec(memory_space=pltpu.VMEM)
    chunks, embeds, weights, sums = [], [], [], []
    done = 0
    stages = gather_rows(feats)
    for s, stage in enumerate(stages):
        items, sums = stage(sums)
        pieces = [piece for piece, _ in items]
        chunks.append([chunk for _, part in items for chunk in part])
        new = sum(piece.shape[0] for piece in pieces)
        state = [((new, width), bf16), ((rows, new), f32), ((8, done + new), f32)]
        final = s == len(stages) - 1
        outs = [((rows, width), f32), ((1, rows), f32)] if final else state + [((rows, rows), f32)]
        operands = [mates, feats, *embeds, *(weights if final else []), *sums, *pieces]
        results = pl.pallas_call(
            functools.partial(stage_kernel, list(chunks), final),
            out_shape=tuple(jax.ShapeDtypeStruct(shape, dtype) for shape, dtype in outs),
            in_specs=[vmem] * len(operands),
            out_specs=(vmem,) * len(outs),
            scratch_shapes=[pltpu.VMEM(shape, dtype) for shape, dtype in (state if final else [])],
            cost_estimate=pl.CostEstimate(flops=1000, bytes_accessed=0, transcendentals=0),
            compiler_params=pltpu.CompilerParams(vmem_limit_bytes=32 * 1024 * 1024),
        )(*operands)
        if not final:
            embeds.append(results[0])
            weights.append(results[1])
            sums = list(results[2:])
        done += new
    grad, loss = results
    return grad, loss.reshape(rows)


def on_device(feats, partner):
    fits = lax.axis_size("batch") == 16 and lax.axis_size("rep") == 2 and feats.shape[0] == 128
    return whole_plan(feats, partner) if fits else split_plan(feats, partner)


def solution(mesh):
    in_specs = (P("batch", None), P("batch"))
    out_specs = (P("batch", None), P("batch"))
    return jax.shard_map(
        on_device, mesh=mesh, in_specs=in_specs, out_specs=out_specs, check_vma=False
    )
```

```python
import functools
import math

import jax
import jax.numpy as jnp
from jax import lax
from jax.experimental import pallas as pl
from jax.experimental.pallas import tpu as pltpu
from jax.sharding import PartitionSpec as P

inv_temp = 10.0
log2e = 1.4426950408889634


def split_plan(feats, partner):
    rows, width = feats.shape
    layers = lax.axis_size("rep")
    share = rows // layers
    layer = lax.axis_index("rep")
    block_index = lax.axis_index("batch")
    hf = feats.astype(jnp.float32)
    scale = lax.rsqrt(jnp.sum(hf * hf, axis=-1, keepdims=True) + 1e-06)
    unit = hf * scale
    embed = unit.astype(jnp.bfloat16)
    own_ids = block_index * rows + jnp.arange(rows, dtype=jnp.int32)
    mine = lax.dynamic_slice_in_dim(embed, layer * share, share, 0)

    def key_ids(start, count):
        gathered = start + jnp.arange(count, dtype=jnp.int32)
        return gathered // share * rows + layer * share + gathered % share

    def first_fold(carry, piece, start):
        denom, pscore = carry
        score = jnp.dot(embed, piece.T, preferred_element_type=jnp.float32) * inv_temp
        ids = key_ids(start, piece.shape[0])
        weight = jnp.where(ids[None, :] == own_ids[:, None], 0.0, jnp.exp(score - inv_temp))
        hits = jnp.where(ids[None, :] == partner[:, None], score, 0.0)
        return (denom + jnp.sum(weight, axis=1), pscore + jnp.sum(hits, axis=1))

    empty_rows = jnp.zeros((rows,), jnp.float32)
    keys = lax.all_gather(mine, "batch", axis=0, tiled=True)
    group = math.gcd(lax.axis_size("batch"), max(1, 512 // share))
    span = group * share
    turns = keys.shape[0] // span
    stacked = keys.reshape(turns, span, width)
    starts = jnp.arange(turns, dtype=jnp.int32) * span

    def first_step(carry, item):
        return (first_fold(carry, item[0], item[1]), None)

    (denom, pscore), unused = lax.scan(first_step, (empty_rows, empty_rows), (stacked, starts))
    denom, pscore = lax.psum((denom, pscore), "rep")
    lse = jnp.log(denom) + inv_temp
    loss = lse - pscore
    lse_share = lax.dynamic_slice_in_dim(lse, layer * share, share, 0)

    def second_fold(acc, pieces, start):
        piece, piece_lse = pieces
        score = jnp.dot(embed, piece.T, preferred_element_type=jnp.float32) * inv_temp
        ids = key_ids(start, piece.shape[0])
        coeff = jnp.exp(score - lse[:, None]) + jnp.exp(score - piece_lse[None, :])
        coeff = coeff - 2.0 * jnp.where(ids[None, :] == partner[:, None], 1.0, 0.0)
        coeff = jnp.where(ids[None, :] == own_ids[:, None], 0.0, coeff).astype(jnp.bfloat16)
        return acc + jnp.dot(coeff, piece, preferred_element_type=jnp.float32)

    empty_acc = jnp.zeros((rows, width), jnp.float32)
    key_lse = lax.all_gather(lse_share, "batch", axis=0, tiled=True)
    stacked_lse = key_lse.reshape(turns, span)

    def second_step(acc, item):
        return (second_fold(acc, (item[0], item[1]), item[2]), None)

    acc, unused = lax.scan(second_step, empty_acc, (stacked, stacked_lse, starts))
    part_sum = lax.psum_scatter(acc, "rep", scatter_dimension=0, tiled=True)
    dz_share = part_sum * inv_temp
    unit_share = lax.dynamic_slice_in_dim(unit, layer * share, share, 0)
    scale_share = lax.dynamic_slice_in_dim(scale, layer * share, share, 0)
    grad_share = scale_share * (
        dz_share - unit_share * jnp.sum(unit_share * dz_share, axis=-1, keepdims=True)
    )
    grad = lax.all_gather(grad_share, "rep", axis=0, tiled=True)
    return (grad, loss)


X, Y, XY, Z1, Z2, Z3 = 1, 2, 3, 4, 8, 12


def send(piece, first, second=None):
    offsets = (first, first if second is None else second)
    pairs = [
        (2 * b + c, 2 * (b ^ offsets[c]) + c) for b in range(lax.axis_size("batch")) for c in range(2)
    ]
    return lax.ppermute(piece, ("batch", "rep"), pairs)


def swap(piece):
    return lax.ppermute(piece, "rep", [(0, 1), (1, 0)])


def join(*pieces):
    return jnp.concatenate(pieces, axis=0)


class Chunk:
    def __init__(self, *offsets):
        self.offsets = offsets

    def swapped(self):
        return Chunk(*self.offsets[::-1])


def tie(*values):
    return lax.optimization_barrier(values)


def gather_rows(feats):
    far = send(feats, Z2, Z3)
    near = send(feats, X, Y)
    cross = send(feats, XY, Z1)
    far, near = tie(far, near)
    side = send(near, Z1)
    side_xy = send(cross, Z1, XY)
    far_x, far_y = send(far, X, Y), send(far, Y, X)
    far_xy = send(far_x, Y, X)
    early = join(near, cross, far)
    pair = join(far_x, far_y)
    early_chunks = [Chunk(X, Y), Chunk(XY, Z1), Chunk(Z2, Z3)]
    pair_chunks = [Chunk(X ^ Z2, Y ^ Z3), Chunk(Y ^ Z2, X ^ Z3)]
    far_xy_chunks = [Chunk(XY ^ Z2, XY ^ Z3)]
    side_chunks = [Chunk(X ^ Z1, Y ^ Z1)]
    held = {}

    def other(piece, chunks):
        return swap(piece), [chunk.swapped() for chunk in chunks]

    def first(sums):
        return [(feats, [Chunk(0, 0)]), (early, early_chunks), other(early, early_chunks), (pair, pair_chunks)], sums

    def second(sums):
        held["side"], piece, hits = tie(side, side_xy, sums[1])
        return [(held["side"], side_chunks), (piece, [Chunk(XY ^ Z1, XY ^ Z1)])], [sums[0], hits]

    def third(sums):
        held["far_xy"], held["side"], hits = tie(far_xy, held["side"], sums[1])
        return [other(pair, pair_chunks), (held["far_xy"], far_xy_chunks)], [sums[0], hits]

    def last(sums):
        piece = held["far_xy"]
        return [other(held["side"], side_chunks), other(piece, far_xy_chunks)], sums

    return [first, second, third, last]


def normalized(raw):
    hf = raw.astype(jnp.float32)
    scale = lax.rsqrt(jnp.sum(hf * hf, axis=-1, keepdims=True) + 1e-06)
    return hf * scale, scale


def normalize_into(embed, refs):
    start = 0
    for ref in refs:
        count = ref.shape[0]
        for at in range(0, count, 64):
            embed[start + at : start + at + 64, :] = normalized(ref[at : at + 64, :])[0].astype(jnp.bfloat16)
        start += count


def partner_column(partner_ref):
    rows = partner_ref.shape[1]
    spread = jnp.broadcast_to(partner_ref[...], (rows, rows)).astype(jnp.float32)
    return jnp.sum(jnp.where(diagonal(rows), spread, 0.0), axis=1, keepdims=True).astype(jnp.int32)


def diagonal(size):
    r = lax.broadcasted_iota(jnp.int32, (size, size), 0)
    c = lax.broadcasted_iota(jnp.int32, (size, size), 1)
    return r == c


def column_ids(chunks, rows):
    layer = lax.axis_index("rep")
    block = lax.axis_index("batch")
    lane = lax.broadcasted_iota(jnp.int32, (1, rows), 1)
    return [lane + (block ^ jnp.where(layer == 0, *chunk.offsets)) * rows for chunk in chunks]


def spans(total, block):
    return [slice(start, min(start + block, total)) for start in range(0, total, block)]


def shift(span, by):
    return slice(span.start + by, span.stop + by)


def weigh(left, right):
    score = lax.dot_general(left, right, (((1,), (1,)), ((), ())), preferred_element_type=jnp.float32)
    return score, jnp.exp2(score * (inv_temp * log2e))


def fold_rows(weight):
    return jnp.sum(weight.reshape(weight.shape[0] // 8, 8, weight.shape[1]), axis=0)


def fold_columns(weight):
    return sum(weight[:, k : k + 128] for k in range(0, weight.shape[1], 128))


def triangle(embed, total, block, denom, top):
    blocks = total // block
    for i in range(blocks):
        left = embed[i * block : (i + 1) * block, :]
        row_sum = jnp.zeros((block, 128), jnp.float32)
        for j in range(i, blocks):
            score, weight = weigh(left, embed[j * block : (j + 1) * block, :])
            if i == j:
                weight = jnp.where(diagonal(block), 0.0, weight)
            else:
                row_sum += fold_columns(weight)
            if i == 0:
                top(j, score, weight)
            denom[:, j * block : (j + 1) * block] += fold_rows(weight)
        if i != blocks - 1:
            denom[:, i * block : (i + 1) * block] += fold_rows(row_sum.T)


def stage_kernel(chunks, final, partner_ref, own_ref, *refs):
    before = chunks[:-1]
    refs = list(refs)

    def take(count):
        taken = refs[:count]
        del refs[:count]
        return taken

    old_embeds = take(len(before))
    old_weights = take(len(before)) if final else []
    old_denom, old_hits = take(2) if before else (None, None)
    if final:
        grad_ref, loss_ref, embed, weights, denom = refs[-5:]
        pieces = refs[:-5]
    else:
        embed, weights, denom, hits_ref = refs[-4:]
        pieces = refs[:-4]
    rows, width = own_ref.shape
    block = 2 * rows
    new = embed.shape[0]
    old = denom.shape[1] - new

    normalize_into(embed, pieces)
    mates = partner_column(partner_ref)
    ids = [column_ids(part, rows) for part in chunks]
    hits = old_hits[...] if before else jnp.zeros((rows, rows), jnp.float32)
    if before:
        denom[:, :old] = old_denom[...]
    denom[:, old:] = jnp.zeros((8, new), jnp.float32)

    def is_mate(names, span):
        return [name == mates for name in names[span.start // rows : span.stop // rows]]

    def found(span, score):
        return sum(
            jnp.where(mate, score[:rows, k * rows : (k + 1) * rows], 0.0)
            for k, mate in enumerate(is_mate(ids[-1], span))
        )

    start = 0
    for old_embed in old_embeds:
        for i in spans(old_embed.shape[0], 2 * block):
            left = old_embed[i, :]
            row_sum = jnp.zeros((left.shape[0], 128), jnp.float32)
            for j in spans(new, block):
                score, weight = weigh(left, embed[j, :])
                if start + i.start == 0:
                    weights[:, j] = weight[:rows]
                    hits += found(j, score)
                row_sum += fold_columns(weight)
                denom[:, shift(j, old)] += fold_rows(weight)
            denom[:, shift(i, start)] += fold_rows(row_sum.T)
        start += old_embed.shape[0]
    small = rows if final and new <= 3 * rows else block
    for i in spans(new, small):
        left = embed[i, :]
        row_sum = jnp.zeros((left.shape[0], 128), jnp.float32)
        for j in spans(new, small):
            if j.start < i.start:
                continue
            score, weight = weigh(left, embed[j, :])
            if i == j:
                weight = jnp.where(diagonal(weight.shape[0]), 0.0, weight)
            else:
                row_sum += fold_columns(weight)
            if not before and i.start == 0:
                weights[:, j] = weight[:rows]
                hits += found(j, score)
            denom[:, shift(j, old)] += fold_rows(weight)
        if i.stop != new:
            denom[:, shift(i, old)] += fold_rows(row_sum.T)
    if not final:
        hits_ref[...] = hits
        return

    all_weights = [*old_weights, weights]
    own = jnp.sum(sum(fold_columns(w[...]) for w in all_weights), axis=1, keepdims=True)
    loss = jnp.log(own) - inv_temp * jnp.sum(hits, axis=1, keepdims=True)
    loss_ref[...] = jnp.sum(jnp.where(diagonal(rows), loss, 0.0), axis=0, keepdims=True)
    own_inverse = 1.0 / own
    dz = jnp.zeros((rows, width), jnp.float32)
    start = 0
    for e, w, names in zip([*old_embeds, embed], all_weights, ids):
        for j in spans(e.shape[0], block):
            inverse = 1.0 / jnp.sum(denom[:, shift(j, start)], axis=0, keepdims=True)
            mate = jnp.concatenate(is_mate(names, j), axis=1)
            coeff = w[:, j] * (own_inverse + inverse) - jnp.where(mate, 2.0, 0.0)
            dz += jnp.dot(coeff.astype(jnp.bfloat16), e[j, :], preferred_element_type=jnp.float32)
        start += e.shape[0]
    dz = dz * inv_temp
    unit, scale = normalized(own_ref[...])
    grad_ref[...] = scale * (dz - unit * jnp.sum(unit * dz, axis=-1, keepdims=True))


def whole_plan(feats, partner):
    rows, width = feats.shape
    mates = partner[None, :]
    f32, bf16 = jnp.float32, jnp.bfloat16
    vmem = pl.BlockSpec(memory_space=pltpu.VMEM)
    chunks, embeds, weights, sums = [], [], [], []
    done = 0
    stages = gather_rows(feats)
    for s, stage in enumerate(stages):
        items, sums = stage(sums)
        pieces = [piece for piece, _ in items]
        chunks.append([chunk for _, part in items for chunk in part])
        new = sum(piece.shape[0] for piece in pieces)
        state = [((new, width), bf16), ((rows, new), f32), ((8, done + new), f32)]
        final = s == len(stages) - 1
        outs = [((rows, width), f32), ((1, rows), f32)] if final else state + [((rows, rows), f32)]
        operands = [mates, feats, *embeds, *(weights if final else []), *sums, *pieces]
        results = pl.pallas_call(
            functools.partial(stage_kernel, list(chunks), final),
            out_shape=tuple(jax.ShapeDtypeStruct(shape, dtype) for shape, dtype in outs),
            in_specs=[vmem] * len(operands),
            out_specs=(vmem,) * len(outs),
            scratch_shapes=[pltpu.VMEM(shape, dtype) for shape, dtype in (state if final else [])],
            cost_estimate=pl.CostEstimate(flops=1000, bytes_accessed=0, transcendentals=0),
            compiler_params=pltpu.CompilerParams(vmem_limit_bytes=32 * 1024 * 1024),
        )(*operands)
        if not final:
            embeds.append(results[0])
            weights.append(results[1])
            sums = list(results[2:])
        done += new
    grad, loss = results
    return grad, loss.reshape(rows)


def on_device(feats, partner):
    fits = lax.axis_size("batch") == 16 and lax.axis_size("rep") == 2 and feats.shape[0] == 128
    return whole_plan(feats, partner) if fits else split_plan(feats, partner)


def solution(mesh):
    in_specs = (P("batch", None), P("batch"))
    out_specs = (P("batch", None), P("batch"))
    return jax.shard_map(
        on_device, mesh=mesh, in_specs=in_specs, out_specs=out_specs, check_vma=False
    )
```

```python
import functools
import math

import jax
import jax.numpy as jnp
from jax import lax
from jax.experimental import pallas as pl
from jax.experimental.pallas import tpu as pltpu
from jax.sharding import PartitionSpec as P

inv_temp = 10.0
log2e = 1.4426950408889634


def split_plan(feats, partner):
    rows, width = feats.shape
    layers = lax.axis_size("rep")
    share = rows // layers
    layer = lax.axis_index("rep")
    block_index = lax.axis_index("batch")
    hf = feats.astype(jnp.float32)
    scale = lax.rsqrt(jnp.sum(hf * hf, axis=-1, keepdims=True) + 1e-06)
    unit = hf * scale
    embed = unit.astype(jnp.bfloat16)
    own_ids = block_index * rows + jnp.arange(rows, dtype=jnp.int32)
    mine = lax.dynamic_slice_in_dim(embed, layer * share, share, 0)

    def key_ids(start, count):
        gathered = start + jnp.arange(count, dtype=jnp.int32)
        return gathered // share * rows + layer * share + gathered % share

    def first_fold(carry, piece, start):
        denom, pscore = carry
        score = jnp.dot(embed, piece.T, preferred_element_type=jnp.float32) * inv_temp
        ids = key_ids(start, piece.shape[0])
        weight = jnp.where(ids[None, :] == own_ids[:, None], 0.0, jnp.exp(score - inv_temp))
        hits = jnp.where(ids[None, :] == partner[:, None], score, 0.0)
        return (denom + jnp.sum(weight, axis=1), pscore + jnp.sum(hits, axis=1))

    empty_rows = jnp.zeros((rows,), jnp.float32)
    keys = lax.all_gather(mine, "batch", axis=0, tiled=True)
    group = math.gcd(lax.axis_size("batch"), max(1, 512 // share))
    span = group * share
    turns = keys.shape[0] // span
    stacked = keys.reshape(turns, span, width)
    starts = jnp.arange(turns, dtype=jnp.int32) * span

    def first_step(carry, item):
        return (first_fold(carry, item[0], item[1]), None)

    (denom, pscore), unused = lax.scan(first_step, (empty_rows, empty_rows), (stacked, starts))
    denom, pscore = lax.psum((denom, pscore), "rep")
    lse = jnp.log(denom) + inv_temp
    loss = lse - pscore
    lse_share = lax.dynamic_slice_in_dim(lse, layer * share, share, 0)

    def second_fold(acc, pieces, start):
        piece, piece_lse = pieces
        score = jnp.dot(embed, piece.T, preferred_element_type=jnp.float32) * inv_temp
        ids = key_ids(start, piece.shape[0])
        coeff = jnp.exp(score - lse[:, None]) + jnp.exp(score - piece_lse[None, :])
        coeff = coeff - 2.0 * jnp.where(ids[None, :] == partner[:, None], 1.0, 0.0)
        coeff = jnp.where(ids[None, :] == own_ids[:, None], 0.0, coeff).astype(jnp.bfloat16)
        return acc + jnp.dot(coeff, piece, preferred_element_type=jnp.float32)

    empty_acc = jnp.zeros((rows, width), jnp.float32)
    key_lse = lax.all_gather(lse_share, "batch", axis=0, tiled=True)
    stacked_lse = key_lse.reshape(turns, span)

    def second_step(acc, item):
        return (second_fold(acc, (item[0], item[1]), item[2]), None)

    acc, unused = lax.scan(second_step, empty_acc, (stacked, stacked_lse, starts))
    part_sum = lax.psum_scatter(acc, "rep", scatter_dimension=0, tiled=True)
    dz_share = part_sum * inv_temp
    unit_share = lax.dynamic_slice_in_dim(unit, layer * share, share, 0)
    scale_share = lax.dynamic_slice_in_dim(scale, layer * share, share, 0)
    grad_share = scale_share * (
        dz_share - unit_share * jnp.sum(unit_share * dz_share, axis=-1, keepdims=True)
    )
    grad = lax.all_gather(grad_share, "rep", axis=0, tiled=True)
    return (grad, loss)


X, Y, XY, Z1, Z2, Z3 = 1, 2, 3, 4, 8, 12


def send(piece, first, second=None):
    offsets = (first, first if second is None else second)
    pairs = [
        (2 * b + c, 2 * (b ^ offsets[c]) + c) for b in range(lax.axis_size("batch")) for c in range(2)
    ]
    return lax.ppermute(piece, ("batch", "rep"), pairs)


def swap(piece):
    return lax.ppermute(piece, "rep", [(0, 1), (1, 0)])


def join(*pieces):
    return jnp.concatenate(pieces, axis=0)


class Chunk:
    def __init__(self, *offsets):
        self.offsets = offsets

    def swapped(self):
        return Chunk(*self.offsets[::-1])


def tie(*values):
    return lax.optimization_barrier(values)


def gather_rows(feats):
    far = send(feats, Z2, Z3)
    near = send(feats, Y, X)
    cross = send(feats, XY, Z1)
    far, near = tie(far, near)
    side = send(near, Z1)
    side_xy = send(cross, Z1, XY)
    far_x, far_y = send(far, Y, X), send(far, X, Y)
    far_xy = send(far_x, X, Y)
    early = join(near, cross, far)
    pair = join(far_x, far_y)
    early_chunks = [Chunk(Y, X), Chunk(XY, Z1), Chunk(Z2, Z3)]
    pair_chunks = [Chunk(Y ^ Z2, X ^ Z3), Chunk(X ^ Z2, Y ^ Z3)]
    far_xy_chunks = [Chunk(XY ^ Z2, XY ^ Z3)]
    side_chunks = [Chunk(Y ^ Z1, X ^ Z1)]
    held = {}

    def other(piece, chunks):
        return swap(piece), [chunk.swapped() for chunk in chunks]

    def first(sums):
        return [(feats, [Chunk(0, 0)]), (early, early_chunks), other(early, early_chunks), (pair, pair_chunks)], sums

    def second(sums):
        held["side"], piece, hits = tie(side, side_xy, sums[1])
        return [(held["side"], side_chunks), (piece, [Chunk(XY ^ Z1, XY ^ Z1)])], [sums[0], hits]

    def third(sums):
        held["far_xy"], held["side"], hits = tie(far_xy, held["side"], sums[1])
        return [(held["far_xy"], far_xy_chunks), other(pair, pair_chunks)], [sums[0], hits]

    def last(sums):
        piece = held["far_xy"]
        return [other(piece, far_xy_chunks), other(held["side"], side_chunks)], sums

    return [first, second, third, last]


def normalized(raw):
    hf = raw.astype(jnp.float32)
    scale = lax.rsqrt(jnp.sum(hf * hf, axis=-1, keepdims=True) + 1e-06)
    return hf * scale, scale


def normalize_into(embed, refs):
    start = 0
    for ref in refs:
        count = ref.shape[0]
        for at in range(0, count, 64):
            embed[start + at : start + at + 64, :] = normalized(ref[at : at + 64, :])[0].astype(jnp.bfloat16)
        start += count


def partner_column(partner_ref):
    rows = partner_ref.shape[1]
    spread = jnp.broadcast_to(partner_ref[...], (rows, rows)).astype(jnp.float32)
    return jnp.sum(jnp.where(diagonal(rows), spread, 0.0), axis=1, keepdims=True).astype(jnp.int32)


def diagonal(size):
    r = lax.broadcasted_iota(jnp.int32, (size, size), 0)
    c = lax.broadcasted_iota(jnp.int32, (size, size), 1)
    return r == c


def column_ids(chunks, rows):
    layer = lax.axis_index("rep")
    block = lax.axis_index("batch")
    lane = lax.broadcasted_iota(jnp.int32, (1, rows), 1)
    return [lane + (block ^ jnp.where(layer == 0, *chunk.offsets)) * rows for chunk in chunks]


def spans(total, block):
    return [slice(start, min(start + block, total)) for start in range(0, total, block)]


def shift(span, by):
    return slice(span.start + by, span.stop + by)


def weigh(left, right):
    score = lax.dot_general(left, right, (((1,), (1,)), ((), ())), preferred_element_type=jnp.float32)
    return score, jnp.exp2(score * (inv_temp * log2e))


def fold_rows(weight):
    return jnp.sum(weight.reshape(weight.shape[0] // 8, 8, weight.shape[1]), axis=0)


def fold_columns(weight):
    return sum(weight[:, k : k + 128] for k in range(0, weight.shape[1], 128))


def triangle(embed, total, block, denom, top):
    blocks = total // block
    for i in range(blocks):
        left = embed[i * block : (i + 1) * block, :]
        row_sum = jnp.zeros((block, 128), jnp.float32)
        for j in range(i, blocks):
            score, weight = weigh(left, embed[j * block : (j + 1) * block, :])
            if i == j:
                weight = jnp.where(diagonal(block), 0.0, weight)
            else:
                row_sum += fold_columns(weight)
            if i == 0:
                top(j, score, weight)
            denom[:, j * block : (j + 1) * block] += fold_rows(weight)
        if i != blocks - 1:
            denom[:, i * block : (i + 1) * block] += fold_rows(row_sum.T)


def stage_kernel(chunks, final, partner_ref, own_ref, *refs):
    before = chunks[:-1]
    refs = list(refs)

    def take(count):
        taken = refs[:count]
        del refs[:count]
        return taken

    old_embeds = take(len(before))
    old_weights = take(len(before)) if final else []
    old_denom, old_hits = take(2) if before else (None, None)
    if final:
        grad_ref, loss_ref, embed, weights, denom = refs[-5:]
        pieces = refs[:-5]
    else:
        embed, weights, denom, hits_ref = refs[-4:]
        pieces = refs[:-4]
    rows, width = own_ref.shape
    block = 2 * rows
    new = embed.shape[0]
    old = denom.shape[1] - new

    normalize_into(embed, pieces)
    mates = partner_column(partner_ref)
    ids = [column_ids(part, rows) for part in chunks]
    hits = old_hits[...] if before else jnp.zeros((rows, rows), jnp.float32)
    if before:
        denom[:, :old] = old_denom[...]
    denom[:, old:] = jnp.zeros((8, new), jnp.float32)

    def is_mate(names, span):
        return [name == mates for name in names[span.start // rows : span.stop // rows]]

    def found(span, score):
        return sum(
            jnp.where(mate, score[:rows, k * rows : (k + 1) * rows], 0.0)
            for k, mate in enumerate(is_mate(ids[-1], span))
        )

    start = 0
    for old_embed in old_embeds:
        for i in spans(old_embed.shape[0], 2 * block):
            left = old_embed[i, :]
            row_sum = jnp.zeros((left.shape[0], 128), jnp.float32)
            for j in spans(new, block):
                score, weight = weigh(left, embed[j, :])
                if start + i.start == 0:
                    weights[:, j] = weight[:rows]
                    hits += found(j, score)
                row_sum += fold_columns(weight)
                denom[:, shift(j, old)] += fold_rows(weight)
            denom[:, shift(i, start)] += fold_rows(row_sum.T)
        start += old_embed.shape[0]
    small = rows if final and new <= 3 * rows else block
    for i in spans(new, small):
        left = embed[i, :]
        row_sum = jnp.zeros((left.shape[0], 128), jnp.float32)
        for j in spans(new, small):
            if j.start < i.start:
                continue
            score, weight = weigh(left, embed[j, :])
            if i == j:
                weight = jnp.where(diagonal(weight.shape[0]), 0.0, weight)
            else:
                row_sum += fold_columns(weight)
            if not before and i.start == 0:
                weights[:, j] = weight[:rows]
                hits += found(j, score)
            denom[:, shift(j, old)] += fold_rows(weight)
        if i.stop != new:
            denom[:, shift(i, old)] += fold_rows(row_sum.T)
    if not final:
        hits_ref[...] = hits
        return

    all_weights = [*old_weights, weights]
    own = jnp.sum(sum(fold_columns(w[...]) for w in all_weights), axis=1, keepdims=True)
    loss = jnp.log(own) - inv_temp * jnp.sum(hits, axis=1, keepdims=True)
    loss_ref[...] = jnp.sum(jnp.where(diagonal(rows), loss, 0.0), axis=0, keepdims=True)
    own_inverse = 1.0 / own
    dz = jnp.zeros((rows, width), jnp.float32)
    start = 0
    for e, w, names in zip([*old_embeds, embed], all_weights, ids):
        for j in spans(e.shape[0], block):
            inverse = 1.0 / jnp.sum(denom[:, shift(j, start)], axis=0, keepdims=True)
            mate = jnp.concatenate(is_mate(names, j), axis=1)
            coeff = w[:, j] * (own_inverse + inverse) - jnp.where(mate, 2.0, 0.0)
            dz += jnp.dot(coeff.astype(jnp.bfloat16), e[j, :], preferred_element_type=jnp.float32)
        start += e.shape[0]
    dz = dz * inv_temp
    unit, scale = normalized(own_ref[...])
    grad_ref[...] = scale * (dz - unit * jnp.sum(unit * dz, axis=-1, keepdims=True))


def whole_plan(feats, partner):
    rows, width = feats.shape
    mates = partner[None, :]
    f32, bf16 = jnp.float32, jnp.bfloat16
    vmem = pl.BlockSpec(memory_space=pltpu.VMEM)
    chunks, embeds, weights, sums = [], [], [], []
    done = 0
    stages = gather_rows(feats)
    for s, stage in enumerate(stages):
        items, sums = stage(sums)
        pieces = [piece for piece, _ in items]
        chunks.append([chunk for _, part in items for chunk in part])
        new = sum(piece.shape[0] for piece in pieces)
        state = [((new, width), bf16), ((rows, new), f32), ((8, done + new), f32)]
        final = s == len(stages) - 1
        outs = [((rows, width), f32), ((1, rows), f32)] if final else state + [((rows, rows), f32)]
        operands = [mates, feats, *embeds, *(weights if final else []), *sums, *pieces]
        results = pl.pallas_call(
            functools.partial(stage_kernel, list(chunks), final),
            out_shape=tuple(jax.ShapeDtypeStruct(shape, dtype) for shape, dtype in outs),
            in_specs=[vmem] * len(operands),
            out_specs=(vmem,) * len(outs),
            scratch_shapes=[pltpu.VMEM(shape, dtype) for shape, dtype in (state if final else [])],
            cost_estimate=pl.CostEstimate(flops=1000, bytes_accessed=0, transcendentals=0),
            compiler_params=pltpu.CompilerParams(vmem_limit_bytes=32 * 1024 * 1024),
        )(*operands)
        if not final:
            embeds.append(results[0])
            weights.append(results[1])
            sums = list(results[2:])
        done += new
    grad, loss = results
    return grad, loss.reshape(rows)


def on_device(feats, partner):
    fits = lax.axis_size("batch") == 16 and lax.axis_size("rep") == 2 and feats.shape[0] == 128
    return whole_plan(feats, partner) if fits else split_plan(feats, partner)


def solution(mesh):
    in_specs = (P("batch", None), P("batch"))
    out_specs = (P("batch", None), P("batch"))
    return jax.shard_map(
        on_device, mesh=mesh, in_specs=in_specs, out_specs=out_specs, check_vma=False
    )
```
